32 devices in a mesh: inst: 8 (over y, x, core), space: 4 (over z).
Axes of the slice: x: 2, y: 2, z: 4, core: 2. Of those that a mesh axis runs over, the one named last changes fastest.
Arguments:
- flow_state: float32 [8, 6, 256, 128], P('inst', None, 'space'), may hold values from -6 to 6
- forcing: float32 [8, 6, 256, 128], P('inst', None, 'space'), may hold values from -6 to 6
- pivot_table: float32 [8, 6, 6, 128], replicated, may hold values from -0.21 to 1, as said below
- block_offset: int32 [256], P('space'), may hold values from 0 to 7
- line_perm: int32 [128], replicated, may hold values from 0 to 127, each once
- axial_jac: float32 [6, 6], replicated, may hold values from -2.5 to 2.5
- radial_jac: float32 [6, 6], replicated, may hold values from -2.5 to 2.5
- lower_block: float32 [6, 6], replicated, may hold values from -0.035 to 0.97, as said below
- upper_block: float32 [6, 6], replicated, may hold values from -0.035 to 0.97, as said below
Outputs:
- residual: float32 [8, 6, 256, 128], P('inst', None, 'space')
- correction: float32 [8, 6, 256, 128], P('inst', None, 'space')
The draws below stay inside these ranges and needn't reach their ends.
Inputs may be any that keep to these rules, and one draw needn't show every extreme that they name: `pivot_table`: diagonal entries lie in 0.6 to 1. `lower_block`: diagonal entries lie in 0.3 to 0.97, the others in -0.035 to 0.035. `upper_block`: diagonal entries lie in 0.3 to 0.97, the others in -0.035 to 0.035.
All inputs are finite; a program needn't handle non-finite values.
Results may differ from the reference program's by a relative error of at most 0.0001.
Values sent between devices are 32-bit elements; how exact they have to be, the bound alone decides.
A program may use at most 64 MiB of HBM per device.

```python
import math
import jax
import jax.numpy as jnp
from jax import lax

NV = 6
NR = 128
KB = 8
NT = 8
NA = 256


def draw_pivot_table(key, part):
    diag_key, off_key = jax.random.split(jax.random.fold_in(key, 17))
    off_values = 0.07 * jax.random.truncated_normal(off_key, -3.0, 3.0, (KB, NV, NV, NR), jnp.float32)
    diag_values = jnp.exp(jax.random.uniform(diag_key, (KB, NV, 1, NR), jnp.float32, math.log(0.6), math.log(1.0)))
    row_index = lax.broadcasted_iota(jnp.int32, (1, NV, NV, 1), 1)
    col_index = lax.broadcasted_iota(jnp.int32, (1, NV, NV, 1), 2)
    return jnp.where(row_index == col_index, diag_values, off_values)


def draw_lower_block(key, part):
    diag_key, off_key = jax.random.split(jax.random.fold_in(key, 29))
    diag_values = jnp.exp(jax.random.uniform(diag_key, (NV, 1), jnp.float32, math.log(0.3), math.log(0.97)))
    off_values = jax.random.uniform(off_key, (NV, NV), jnp.float32, -0.035, 0.035)
    row_index = lax.broadcasted_iota(jnp.int32, (NV, NV), 0)
    col_index = lax.broadcasted_iota(jnp.int32, (NV, NV), 1)
    return jnp.where(row_index == col_index, diag_values, off_values)


def draw_upper_block(key, part):
    diag_key, off_key = jax.random.split(jax.random.fold_in(key, 43))
    diag_values = jnp.exp(jax.random.uniform(diag_key, (NV, 1), jnp.float32, math.log(0.3), math.log(0.97)))
    off_values = jax.random.uniform(off_key, (NV, NV), jnp.float32, -0.035, 0.035)
    row_index = lax.broadcasted_iota(jnp.int32, (NV, NV), 0)
    col_index = lax.broadcasted_iota(jnp.int32, (NV, NV), 1)
    return jnp.where(row_index == col_index, diag_values, off_values)


def plant(entries, stream_key, low, high):
    index_at = [jax.random.randint(jax.random.fold_in(stream_key, axis), (), 0, length) for axis, length in enumerate(entries.shape)]
    main_axis = entries.shape.index(max(entries.shape))
    next_to = index_at[:main_axis] + [(index_at[main_axis] + 1) % entries.shape[main_axis]] + index_at[main_axis + 1:]
    return entries.at[tuple(index_at)].set(low).at[tuple(next_to)].set(high)


def levels(stream_key, dims, cuts, least, high):
    factor_of, own = 1.0, jax.random.fold_in(stream_key, 6)
    for dim, parts in cuts:
        steps = jnp.exp(jax.random.uniform(jax.random.fold_in(own, dim), (parts,), jnp.float32, least / len(cuts), high / len(cuts)))
        factor_of = factor_of * jnp.repeat(steps, dims[dim] // parts).reshape([-1 if axis == dim else 1 for axis in range(len(dims))])
    return factor_of


def gaussian(key, shape, deviation, reach, cuts=(), dtype=jnp.bfloat16):
    level = levels(key, shape, cuts, -0.22, 0.18) if cuts else 1.0
    result = jax.random.normal(key, shape, jnp.float32) * deviation * level
    return jnp.minimum(jnp.maximum(result, -reach), reach).astype(dtype)


def setup_inputs(seed: int = 0) -> dict:
    arg_keys = jax.random.split(jax.random.key(seed), 10)
    flow_state = gaussian(arg_keys[0], (NT, NV, NA, NR), 1.0, 6.0, ((0, 8), (2, 4)), jnp.float32)
    forcing = gaussian(arg_keys[1], (NT, NV, NA, NR), 1.0, 6.0, ((0, 8), (2, 4)), jnp.float32)
    pivot_table = draw_pivot_table(jax.random.fold_in(arg_keys[9], 71), 0)
    block_offset = plant(jax.random.randint(arg_keys[3], (NA,), 0, KB), jax.random.fold_in(arg_keys[3], 1), 0, KB - 1).astype(jnp.int32)
    line_perm = jax.random.permutation(arg_keys[4], NR).astype(jnp.int32)
    axial_jac = gaussian(arg_keys[5], (NV, NV), NV ** -0.5, 2.5, (), jnp.float32)
    radial_jac = gaussian(arg_keys[6], (NV, NV), NV ** -0.5, 2.5, (), jnp.float32)
    lower_block = draw_lower_block(jax.random.fold_in(arg_keys[9], 71), 0)
    upper_block = draw_upper_block(jax.random.fold_in(arg_keys[9], 71), 0)
    return dict(flow_state=flow_state, forcing=forcing, pivot_table=pivot_table, block_offset=block_offset, line_perm=line_perm, axial_jac=axial_jac, radial_jac=radial_jac, lower_block=lower_block, upper_block=upper_block)


frequency = 0.5
viscosity = 0.01
damping = 0.25


def spectral_matrix(count):
    row_index = lax.broadcasted_iota(jnp.int32, (count, count), 0)
    col_index = lax.broadcasted_iota(jnp.int32, (count, count), 1)
    distance = row_index - col_index
    parity = (1 - 2 * jnp.mod(distance, 2)).astype(jnp.float32)
    phase_angle = jnp.pi * distance.astype(jnp.float32) / count
    diagonal_mask = distance == 0
    sine_value = jnp.where(diagonal_mask, 1.0, jnp.sin(phase_angle))
    first_order = jnp.where(diagonal_mask, 0.0, 0.5 * parity * jnp.cos(phase_angle) / sine_value)
    second_order = jnp.where(diagonal_mask, -(count * count + 2) / 12.0, -0.5 * parity / (sine_value * sine_value))
    return (frequency * first_order - viscosity * second_order).astype(jnp.float32)


def reference(flow_state, forcing, pivot_table, block_offset, line_perm, axial_jac, radial_jac, lower_block, upper_block):
    hp = lax.Precision.HIGHEST
    line_state = jnp.take(flow_state, line_perm, axis=3)
    line_forcing = jnp.take(forcing, line_perm, axis=3)
    spectral = spectral_matrix(NT)
    timed = jnp.einsum('nm,mvar->nvar', spectral, line_state, precision=hp)
    axial_padded = jnp.pad(line_state, ((0, 0), (0, 0), (1, 1), (0, 0)))
    radial_padded = jnp.pad(line_state, ((0, 0), (0, 0), (0, 0), (1, 1)))
    axial_ahead = axial_padded[:, :, 2:]
    axial_behind = axial_padded[:, :, :-2]
    radial_outer = radial_padded[..., 2:]
    radial_inner = radial_padded[..., :-2]
    flux_terms = jnp.einsum('vw,nwar->nvar', axial_jac, 0.5 * (axial_ahead - axial_behind), precision=hp)
    flux_terms = flux_terms + jnp.einsum('vw,nwar->nvar', radial_jac, 0.5 * (radial_outer - radial_inner), precision=hp)
    residual = flux_terms - damping * (axial_ahead + axial_behind + radial_outer + radial_inner - 4.0 * line_state) + timed - line_forcing
    factors = jnp.take(pivot_table, block_offset, axis=0)
    stacked = jnp.transpose(factors, (3, 1, 2, 0))
    residual_lines = jnp.transpose(residual, (3, 0, 1, 2))

    def forward(previous, element):
        factor, target = element
        inside = target - jnp.einsum('vw,nwa->nva', lower_block, previous, precision=hp)
        current = jnp.einsum('vwa,nwa->nva', factor, inside, precision=hp)
        return current, current

    initial = jnp.zeros((NT, NV, NA), jnp.float32)
    _, forward_sweep = lax.scan(forward, initial, (stacked, residual_lines))

    def backward(following, element):
        factor, partial_value = element
        coupled = jnp.einsum('vw,nwa->nva', upper_block, following, precision=hp)
        current = partial_value - jnp.einsum('vwa,nwa->nva', factor, coupled, precision=hp)
        return current, current

    _, backward_sweep = lax.scan(backward, initial, (stacked, forward_sweep), reverse=True)
    correction = jnp.transpose(backward_sweep, (1, 2, 3, 0))
    return residual, correction
```

```python
import functools

import jax
import jax.numpy as jnp
import numpy as np
from jax import lax
from jax.experimental import pallas as pl
from jax.experimental.pallas import tpu as pltpu
from jax.sharding import PartitionSpec as P

frequency = 0.5
viscosity = 0.01
damping = 0.25

f32 = jnp.float32
MESH = pl.DeviceIdType.MESH
NV = 6
NP = NV // 2
SEG = 8


def spectral_matrix(count):
    index = np.arange(count)
    distance = index[:, None] - index[None, :]
    parity = 1.0 - 2.0 * (distance % 2)
    angle = np.pi * distance / count
    diagonal = distance == 0
    sine = np.where(diagonal, 1.0, np.sin(angle))
    first = np.where(diagonal, 0.0, 0.5 * parity * np.cos(angle) / sine)
    second = np.where(diagonal, -(count * count + 2) / 12.0, -0.5 * parity / (sine * sine))
    return (frequency * first - viscosity * second).astype(np.float32)


def select_columns(x, onehot):
    high = x.astype(jnp.bfloat16)
    rest = x - high.astype(f32)
    middle = rest.astype(jnp.bfloat16)
    low = (rest - middle.astype(f32)).astype(jnp.bfloat16)
    out = jnp.dot(high, onehot, preferred_element_type=f32)
    out = out + jnp.dot(middle, onehot, preferred_element_type=f32)
    return out + jnp.dot(low, onehot, preferred_element_type=f32)


def kernel(
    count,
    spaces,
    state,
    forcing,
    pivot,
    offset,
    perm,
    ajac,
    rjac,
    lower,
    upper,
    res_out,
    cor_out,
    line,
    base,
    send1,
    recv1,
    send2,
    recv2,
    halo_out,
    halo_in,
    tab,
    coef,
    trans,
    rhs,
    sweep0,
    sweep1,
    ssem1,
    rsem1,
    ssem2,
    rsem2,
    hssem,
    hrsem,
):
    stations, radial = state.shape[1], state.shape[2]
    per = stations // count
    steps = radial // SEG
    spectral = spectral_matrix(count)
    me = lax.axis_index("inst")
    here = lax.axis_index("space")
    up = lax.rem(here + 1, spaces)
    down = lax.rem(here + spaces - 1, spaces)

    barrier = pltpu.get_barrier_semaphore()
    for d in range(1, count):
        pl.semaphore_signal(
            barrier, inc=1, device_id={"inst": lax.rem(me + d, count)}, device_id_type=MESH
        )
    for other in (up, down):
        pl.semaphore_signal(barrier, inc=1, device_id={"space": other}, device_id_type=MESH)

    rows = lax.broadcasted_iota(jnp.int32, (radial, radial), 0)
    order = (rows == perm[...]).astype(f32).astype(jnp.bfloat16)
    flat = select_columns(state[...].reshape(NV * stations, radial), order)
    for v in range(NV):
        block = flat[v * stations : (v + 1) * stations]
        line[v, 8 : 8 + stations, :] = block
        halo_out[0, v : v + 1, :] = block[0:1]
        halo_out[1, v : v + 1, :] = block[stations - 1 : stations]
        for e in range(count):
            send1[e, v * per : (v + 1) * per, :] = block[e * per : (e + 1) * per]

    pl.semaphore_wait(barrier, count + 1)

    def exchange(source, target, ssem, rsem):
        copies = []
        for d in range(count - 1, 0, -1):
            other = lax.rem(me + d, count)
            copies.append(
                pltpu.make_async_remote_copy(
                    src_ref=source.at[other],
                    dst_ref=target.at[me],
                    send_sem=ssem.at[d - 1],
                    recv_sem=rsem.at[d - 1],
                    device_id={"inst": other},
                    device_id_type=MESH,
                )
            )
        return copies

    first = exchange(send1, recv1, ssem1, rsem1)
    for copy in first:
        copy.start()
    halos = []
    for side, other in ((0, down), (1, up)):
        halos.append(
            pltpu.make_async_remote_copy(
                src_ref=halo_out.at[side],
                dst_ref=halo_in.at[side],
                send_sem=hssem.at[side],
                recv_sem=hrsem.at[side],
                device_id={"space": other},
                device_id_type=MESH,
            )
        )
    for copy in halos:
        copy.start()
    recv1[me] = send1[me]

    def place(kind, v, w):
        p, h = v // 2, v % 2
        q, crossed = w // 2, (v % 2) ^ (w % 2)
        return ((((kind * NP + p) * NP + q) * 2 + crossed) * 2 + h) * 8

    tab[...] = jnp.zeros_like(tab)
    for v in range(NV):
        for k in range(8):
            block = pivot[k, v]
            for w in range(NV):
                at = place(0, v, w) + k
                tab[at : at + 1, :] = block[w : w + 1, :]
    for kind, matrix in ((1, lower), (2, upper)):
        for v in range(NV):
            parts = [tab[place(0, v, u) : place(0, v, u) + 8, :] for u in range(NV)]
            for w in range(NV):
                total = parts[0] * matrix[0, w]
                for u in range(1, NV):
                    total = total + parts[u] * matrix[u, w]
                at = place(kind, v, w)
                tab[at : at + 8, :] = -total

    lane = lax.broadcasted_iota(jnp.int32, (128, 256), 1)
    row = lax.broadcasted_iota(jnp.int32, (128, 256), 0)
    wanted = offset[...]
    for g in range(4):
        hit = (row - 32 * g == (lane // 64) * 8 + wanted)
        rhs[g] = hit.astype(f32).astype(jnp.bfloat16)

    def expand(b, carry):
        block = tab[pl.ds(pl.multiple_of(b * 128, 128), 128), :].T
        for g in range(4):
            both = select_columns(block, rhs[g])
            coef[b * 8 + 2 * g] = both[:, :128]
            coef[b * 8 + 2 * g + 1] = both[:, 128:]
        return carry

    lax.fori_loop(0, tab.shape[0] // 128, expand, 0)

    def at_step(t):
        return pl.ds(t, SEG, stride=steps)

    def crossed(pairs):
        return [pltpu.roll(x, 64, 1) for x in pairs]

    def apply(coefs, pairs, turned, start=None):
        out = []
        for p in range(NP):
            total = None if start is None else start[p]
            for q in range(NP):
                term = coefs[p][q][0] * pairs[q] + coefs[p][q][1] * turned[q]
                total = term if total is None else total + term
            out.append(total)
        return out

    def load_coefs(kind, t):
        return [
            [
                [coef[((kind * NP + p) * NP + q) * 2 + c, at_step(t), :] for c in range(2)]
                for q in range(NP)
            ]
            for p in range(NP)
        ]

    half = lax.broadcasted_iota(jnp.int32, (SEG, 128), 1) // 64
    unit = [
        [jnp.where(2 * q + half == u, 1.0, 0.0).astype(f32) for q in range(NP)] for u in range(NV)
    ]
    for kind in (0, 1):

        def transfer(i, columns):
            t = i if kind == 0 else steps - 1 - i
            coefs = load_coefs(kind + 1, t)
            new = []
            for u in range(NV):
                got = apply(coefs, columns[u], crossed(columns[u]))
                for p in range(NP):
                    trans[(kind * NV + u) * NP + p, at_step(t), :] = got[p]
                new.append(got)
            return new

        lax.fori_loop(0, steps, transfer, unit)

    order_forcing = select_columns(forcing[...].reshape(NV * stations, radial), order)
    for copy in halos:
        copy.wait_recv()
    for v in range(NV):
        line[v, 8 + stations : 9 + stations, :] = jnp.where(
            here == spaces - 1, 0.0, halo_in[0, v : v + 1, :]
        )
        line[v, 7:8, :] = jnp.where(here == 0, 0.0, halo_in[1, v : v + 1, :])

    spot = lax.broadcasted_iota(jnp.int32, (8, radial), 1)

    def local(i, carry):
        at = pl.multiple_of(i * 8, 8)
        axial, outward, mean = [], [], []
        for v in range(NV):
            window = line[v, pl.ds(at, 24), :]
            centre = window[8:16]
            ahead = window[9:17]
            behind = window[7:15]
            outer = jnp.where(spot == radial - 1, 0.0, pltpu.roll(centre, radial - 1, 1))
            inner = jnp.where(spot == 0, 0.0, pltpu.roll(centre, 1, 1))
            axial.append(0.5 * (ahead - behind))
            outward.append(0.5 * (outer - inner))
            mean.append(damping * (ahead + behind + outer + inner - 4.0 * centre))
        for v in range(NV):
            total = ajac[v, 0] * axial[0] + rjac[v, 0] * outward[0]
            for w in range(1, NV):
                total = total + (ajac[v, w] * axial[w] + rjac[v, w] * outward[w])
            base[v, pl.ds(at, 8), :] = total - mean[v]
        return carry

    lax.fori_loop(0, stations // 8, local, 0)
    for v in range(NV):
        base[v] = base[v] - order_forcing[v * stations : (v + 1) * stations]

    for copy in first:
        copy.wait_recv()
    for n in range(count):
        total = float(spectral[n, 0]) * recv1[0]
        for m in range(1, count):
            total = total + float(spectral[n, m]) * recv1[m]
        send2[n] = total
    second = exchange(send2, recv2, ssem2, rsem2)
    for copy in second:
        copy.start()
    recv2[me] = send2[me]
    for copy in second:
        copy.wait_recv()

    pairs = []
    for p in range(NP):
        blocks = []
        for v in (2 * p, 2 * p + 1):
            timed = jnp.concatenate(
                [recv2[e, v * per : (v + 1) * per, :] for e in range(count)], axis=0
            )
            residual = base[v] + timed
            res_out[v] = residual
            blocks.append(residual)
        sweep0[p] = jnp.concatenate(blocks, axis=0).T

    zeros = [jnp.zeros((SEG, 128), f32) for _ in range(NP)]
    segment = lax.broadcasted_iota(jnp.int32, (SEG, 128), 0)

    def spread(pairs):
        turned = crossed(pairs)
        out = []
        for q in range(NP):
            out.append(jnp.where(half == 0, pairs[q], turned[q]))
            out.append(jnp.where(half == 0, turned[q], pairs[q]))
        return out

    def add_transfer(kind, t, start, spreaded):
        out = []
        for p in range(NP):
            total = start[p]
            for u in range(NV):
                total = total + trans[(kind * NV + u) * NP + p, at_step(t), :] * spreaded[u]
            out.append(total)
        return out

    def carries(kind, last, ends):
        def turn(i, held):
            got = add_transfer(kind, last, ends, spread(held))
            shift, edge = (1, 0) if kind == 0 else (SEG - 1, SEG - 1)
            return [jnp.where(segment == edge, 0.0, pltpu.roll(x, shift, 0)) for x in got]

        return spread(lax.fori_loop(0, SEG - 1, turn, zeros))

    def forward(t, held):
        source = [sweep0[p, at_step(t), :] for p in range(NP)]
        start = apply(load_coefs(0, t), source, crossed(source))
        got = apply(load_coefs(1, t), held, crossed(held), start)
        for p in range(NP):
            sweep1[p, at_step(t), :] = got[p]
        return got

    ends = lax.fori_loop(0, steps, forward, zeros)
    entering = carries(0, steps - 1, ends)

    def backward(i, held):
        t = steps - 1 - i
        start = add_transfer(0, t, [sweep1[p, at_step(t), :] for p in range(NP)], entering)
        got = apply(load_coefs(2, t), held, crossed(held), start)
        for p in range(NP):
            sweep0[p, at_step(t), :] = got[p]
        return got

    ends = lax.fori_loop(0, steps, backward, zeros)
    leaving = carries(1, 0, ends)

    def finish(t, carry):
        got = add_transfer(1, t, [sweep0[p, at_step(t), :] for p in range(NP)], leaving)
        for p in range(NP):
            sweep1[p, at_step(t), :] = got[p]
        return carry

    lax.fori_loop(0, steps, finish, 0)
    for p in range(NP):
        block = sweep1[p].T
        cor_out[2 * p] = block[:stations]
        cor_out[2 * p + 1] = block[stations:]

    for copy in first + halos + second:
        copy.wait_send()


def shards(
    count,
    spaces,
    flow_state,
    forcing,
    pivot_table,
    block_offset,
    line_perm,
    axial_jac,
    radial_jac,
    lower_block,
    upper_block,
):
    _, variables, stations, radial = flow_state.shape
    per = stations // count
    block = jax.ShapeDtypeStruct((variables, stations, radial), f32)
    vmem = pl.BlockSpec(memory_space=pltpu.VMEM)
    smem = pl.BlockSpec(memory_space=pltpu.SMEM)
    dma = pltpu.SemaphoreType.DMA
    exchanged = pltpu.VMEM((count, variables * per, radial), f32)
    residual, correction = pl.pallas_call(
        functools.partial(kernel, count, spaces),
        out_shape=(block, block),
        in_specs=[vmem] * 5 + [smem] * 4,
        out_specs=(vmem, vmem),
        scratch_shapes=[
            pltpu.VMEM((variables, stations + 16, radial), f32),
            pltpu.VMEM((variables, stations, radial), f32),
            exchanged,
            exchanged,
            exchanged,
            exchanged,
            pltpu.VMEM((2, variables, radial), f32),
            pltpu.VMEM((2, variables, radial), f32),
            pltpu.VMEM((896, radial), f32),
            pltpu.VMEM((56, radial, 128), f32),
            pltpu.VMEM((36, radial, 128), f32),
            pltpu.VMEM((4, 128, 256), jnp.bfloat16),
            pltpu.VMEM((NP, radial, 128), f32),
            pltpu.VMEM((NP, radial, 128), f32),
            dma((count - 1,)),
            dma((count - 1,)),
            dma((count - 1,)),
            dma((count - 1,)),
            dma((2,)),
            dma((2,)),
        ],
        compiler_params=pltpu.CompilerParams(
            collective_id=0, has_side_effects=True, vmem_limit_bytes=40 * 1024 * 1024
        ),
    )(
        flow_state[0],
        forcing[0],
        pivot_table,
        jnp.tile(block_offset, 4).reshape(1, 4 * stations),
        line_perm.reshape(1, radial),
        axial_jac,
        radial_jac,
        lower_block,
        upper_block,
    )
    return residual[None], correction[None]


def solution(mesh):
    spec = P("inst", None, "space", None)
    return jax.shard_map(
        functools.partial(shards, mesh.shape["inst"], mesh.shape["space"]),
        mesh=mesh,
        in_specs=(spec, spec, P(), P("space"), P(), P(), P(), P(), P()),
        out_specs=(spec, spec),
        check_vma=False,
    )
```

```python
import functools

import jax
import jax.numpy as jnp
import numpy as np
from jax import lax
from jax.experimental import pallas as pl
from jax.experimental.pallas import tpu as pltpu
from jax.sharding import PartitionSpec as P

frequency = 0.5
viscosity = 0.01
damping = 0.25

f32 = jnp.float32
MESH = pl.DeviceIdType.MESH
NV = 6
NP = NV // 2
SEG = 8


def spectral_matrix(count):
    index = np.arange(count)
    distance = index[:, None] - index[None, :]
    parity = 1.0 - 2.0 * (distance % 2)
    angle = np.pi * distance / count
    diagonal = distance == 0
    sine = np.where(diagonal, 1.0, np.sin(angle))
    first = np.where(diagonal, 0.0, 0.5 * parity * np.cos(angle) / sine)
    second = np.where(diagonal, -(count * count + 2) / 12.0, -0.5 * parity / (sine * sine))
    return (frequency * first - viscosity * second).astype(np.float32)


def select_columns(x, onehot):
    high = x.astype(jnp.bfloat16)
    rest = x - high.astype(f32)
    middle = rest.astype(jnp.bfloat16)
    low = (rest - middle.astype(f32)).astype(jnp.bfloat16)
    out = jnp.dot(high, onehot, preferred_element_type=f32)
    out = out + jnp.dot(middle, onehot, preferred_element_type=f32)
    return out + jnp.dot(low, onehot, preferred_element_type=f32)


def kernel(
    count,
    spaces,
    state_in,
    forcing_in,
    pivot_in,
    offset_in,
    perm_in,
    ajac_in,
    rjac_in,
    lower_in,
    upper_in,
    res_out,
    cor_out,
    state,
    forcing,
    pivot,
    offset,
    perm,
    ajac,
    rjac,
    lower,
    upper,
    insem,
    line,
    base,
    send1,
    recv1,
    send2,
    recv2,
    halo_out,
    halo_in,
    tab,
    coef,
    trans,
    rhs,
    sweep0,
    sweep1,
    ssem1,
    rsem1,
    ssem2,
    rsem2,
    hssem,
    hrsem,
):
    sources = (
        perm_in, state_in, pivot_in, offset_in, lower_in, upper_in, ajac_in, rjac_in, forcing_in
    )
    targets = (perm, state, pivot, offset, lower, upper, ajac, rjac, forcing)
    loads = [
        pltpu.make_async_copy(source, target, insem.at[i])
        for i, (source, target) in enumerate(zip(sources, targets))
    ]
    for load in loads:
        load.start()
    stations, radial = state.shape[1], state.shape[2]
    per = stations // count
    steps = radial // SEG
    spectral = spectral_matrix(count)
    me = lax.axis_index("inst")
    here = lax.axis_index("space")
    up = lax.rem(here + 1, spaces)
    down = lax.rem(here + spaces - 1, spaces)

    barrier = pltpu.get_barrier_semaphore()
    for d in range(1, count):
        pl.semaphore_signal(
            barrier, inc=1, device_id={"inst": lax.rem(me + d, count)}, device_id_type=MESH
        )
    for other in (up, down):
        pl.semaphore_signal(barrier, inc=1, device_id={"space": other}, device_id_type=MESH)

    loads[0].wait()
    rows = lax.broadcasted_iota(jnp.int32, (radial, radial), 0)
    order = (rows == perm[...]).astype(f32).astype(jnp.bfloat16)
    loads[1].wait()
    flat = select_columns(state[...].reshape(NV * stations, radial), order)
    for v in range(NV):
        block = flat[v * stations : (v + 1) * stations]
        line[v, 8 : 8 + stations, :] = block
        halo_out[0, v : v + 1, :] = block[0:1]
        halo_out[1, v : v + 1, :] = block[stations - 1 : stations]
        for e in range(count):
            send1[e, v * per : (v + 1) * per, :] = block[e * per : (e + 1) * per]

    pl.semaphore_wait(barrier, count + 1)

    def exchange(source, target, ssem, rsem):
        copies = []
        for d in range(count - 1, 0, -1):
            other = lax.rem(me + d, count)
            copies.append(
                pltpu.make_async_remote_copy(
                    src_ref=source.at[other],
                    dst_ref=target.at[me],
                    send_sem=ssem.at[d - 1],
                    recv_sem=rsem.at[d - 1],
                    device_id={"inst": other},
                    device_id_type=MESH,
                )
            )
        return copies

    first = exchange(send1, recv1, ssem1, rsem1)
    for copy in first:
        copy.start()
    halos = []
    for side, other in ((0, down), (1, up)):
        halos.append(
            pltpu.make_async_remote_copy(
                src_ref=halo_out.at[side],
                dst_ref=halo_in.at[side],
                send_sem=hssem.at[side],
                recv_sem=hrsem.at[side],
                device_id={"space": other},
                device_id_type=MESH,
            )
        )
    for copy in halos:
        copy.start()
    recv1[me] = send1[me]

    def place(kind, v, w):
        p, h = v // 2, v % 2
        q, crossed = w // 2, (v % 2) ^ (w % 2)
        return ((((kind * NP + p) * NP + q) * 2 + crossed) * 2 + h) * 8

    for load in loads[2:]:
        load.wait()
    tab[864:, :] = jnp.zeros((32, radial), f32)
    for v in range(NV):
        for w in range(NV):
            at = place(0, v, w)
            tab[at : at + 8, :] = pivot[v, w]
    for kind, matrix in ((1, lower), (2, upper)):
        for v in range(NV):
            parts = [pivot[v, u] for u in range(NV)]
            for w in range(NV):
                total = parts[0] * matrix[0, w]
                for u in range(1, NV):
                    total = total + parts[u] * matrix[u, w]
                at = place(kind, v, w)
                tab[at : at + 8, :] = -total

    lane = lax.broadcasted_iota(jnp.int32, (256, 256), 1)
    row = lax.broadcasted_iota(jnp.int32, (256, 256), 0) % 128
    wanted = jnp.concatenate([offset[...]] * 4, axis=1)
    for g in range(4):
        hit = (row - 32 * g == (lane // 64) * 8 + wanted)
        rhs[g] = hit.astype(f32).astype(jnp.bfloat16)

    def expand(b, carry):
        block = tab[pl.ds(pl.multiple_of(b * 128, 128), 128), :].T
        high = block.astype(jnp.bfloat16)
        low = (block - high.astype(f32)).astype(jnp.bfloat16)
        pieces = jnp.concatenate([high, low], axis=1)
        for g in range(4):
            both = jnp.dot(pieces, rhs[g], preferred_element_type=f32)
            coef[b * 8 + 2 * g] = both[:, :128]
            coef[b * 8 + 2 * g + 1] = both[:, 128:]
        return carry

    lax.fori_loop(0, tab.shape[0] // 128, expand, 0)

    def at_step(t):
        return pl.ds(t, SEG, stride=steps)

    def crossed(pairs):
        return [pltpu.roll(x, 64, 1) for x in pairs]

    def apply(coefs, pairs, turned, start=None):
        out = []
        for p in range(NP):
            total = None if start is None else start[p]
            for q in range(NP):
                term = coefs[p][q][0] * pairs[q] + coefs[p][q][1] * turned[q]
                total = term if total is None else total + term
            out.append(total)
        return out

    def load_coefs(kind, t):
        return [
            [
                [coef[((kind * NP + p) * NP + q) * 2 + c, at_step(t), :] for c in range(2)]
                for q in range(NP)
            ]
            for p in range(NP)
        ]

    for copy in first:
        copy.wait_recv()
    for n in range(count):
        total = float(spectral[n, 0]) * recv1[0]
        for m in range(1, count):
            total = total + float(spectral[n, m]) * recv1[m]
        send2[n] = total
    second = exchange(send2, recv2, ssem2, rsem2)
    for copy in second:
        copy.start()
    recv2[me] = send2[me]
    half = lax.broadcasted_iota(jnp.int32, (SEG, 128), 1) // 64
    unit = [
        [jnp.where(2 * q + half == u, 1.0, 0.0).astype(f32) for q in range(NP)] for u in range(NV)
    ]
    for kind in (0, 1):

        def transfer(i, columns):
            t = i if kind == 0 else steps - 1 - i
            coefs = load_coefs(kind + 1, t)
            new = []
            for u in range(NV):
                got = apply(coefs, columns[u], crossed(columns[u]))
                for p in range(NP):
                    trans[(kind * NV + u) * NP + p, at_step(t), :] = got[p]
                new.append(got)
            return new

        lax.fori_loop(0, steps, transfer, unit, unroll=2)

    order_forcing = select_columns(forcing[...].reshape(NV * stations, radial), order)
    for copy in halos:
        copy.wait_recv()
    for v in range(NV):
        line[v, 8 + stations : 9 + stations, :] = jnp.where(
            here == spaces - 1, 0.0, halo_in[0, v : v + 1, :]
        )
        line[v, 7:8, :] = jnp.where(here == 0, 0.0, halo_in[1, v : v + 1, :])

    spot = lax.broadcasted_iota(jnp.int32, (8, radial), 1)

    def local(i, carry):
        at = pl.multiple_of(i * 8, 8)
        axial, outward, mean = [], [], []
        for v in range(NV):
            window = line[v, pl.ds(at, 24), :]
            centre = window[8:16]
            ahead = window[9:17]
            behind = window[7:15]
            outer = jnp.where(spot == radial - 1, 0.0, pltpu.roll(centre, radial - 1, 1))
            inner = jnp.where(spot == 0, 0.0, pltpu.roll(centre, 1, 1))
            axial.append(0.5 * (ahead - behind))
            outward.append(0.5 * (outer - inner))
            mean.append(damping * (ahead + behind + outer + inner - 4.0 * centre))
        for v in range(NV):
            total = ajac[v, 0] * axial[0] + rjac[v, 0] * outward[0]
            for w in range(1, NV):
                total = total + (ajac[v, w] * axial[w] + rjac[v, w] * outward[w])
            base[v, pl.ds(at, 8), :] = total - mean[v]
        return carry

    lax.fori_loop(0, stations // 8, local, 0)
    for v in range(NV):
        base[v] = base[v] - order_forcing[v * stations : (v + 1) * stations]

    for copy in second:
        copy.wait_recv()

    pairs = []
    for p in range(NP):
        blocks = []
        for v in (2 * p, 2 * p + 1):
            timed = jnp.concatenate(
                [recv2[e, v * per : (v + 1) * per, :] for e in range(count)], axis=0
            )
            residual = base[v] + timed
            res_out[v] = residual
            blocks.append(residual)
        sweep0[p] = jnp.concatenate(blocks, axis=0).T

    zeros = [jnp.zeros((SEG, 128), f32) for _ in range(NP)]
    segment = lax.broadcasted_iota(jnp.int32, (SEG, 128), 0)

    def spread(pairs):
        turned = crossed(pairs)
        out = []
        for q in range(NP):
            out.append(jnp.where(half == 0, pairs[q], turned[q]))
            out.append(jnp.where(half == 0, turned[q], pairs[q]))
        return out

    def add_transfer(kind, t, start, spreaded):
        out = []
        for p in range(NP):
            total = start[p]
            for u in range(NV):
                total = total + trans[(kind * NV + u) * NP + p, at_step(t), :] * spreaded[u]
            out.append(total)
        return out

    def carries(kind, last, ends):
        def turn(i, held):
            got = add_transfer(kind, last, ends, spread(held))
            shift, edge = (1, 0) if kind == 0 else (SEG - 1, SEG - 1)
            return [jnp.where(segment == edge, 0.0, pltpu.roll(x, shift, 0)) for x in got]

        return spread(lax.fori_loop(0, SEG - 1, turn, zeros, unroll=True))

    def forward(t, held):
        source = [sweep0[p, at_step(t), :] for p in range(NP)]
        start = apply(load_coefs(0, t), source, crossed(source))
        got = apply(load_coefs(1, t), held, crossed(held), start)
        for p in range(NP):
            sweep1[p, at_step(t), :] = got[p]
        return got

    ends = lax.fori_loop(0, steps, forward, zeros, unroll=4)
    entering = carries(0, steps - 1, ends)

    def backward(i, held):
        t = steps - 1 - i
        start = add_transfer(0, t, [sweep1[p, at_step(t), :] for p in range(NP)], entering)
        got = apply(load_coefs(2, t), held, crossed(held), start)
        for p in range(NP):
            sweep0[p, at_step(t), :] = got[p]
        return got

    ends = lax.fori_loop(0, steps, backward, zeros, unroll=4)
    leaving = carries(1, 0, ends)

    def finish(t, carry):
        got = add_transfer(1, t, [sweep0[p, at_step(t), :] for p in range(NP)], leaving)
        for p in range(NP):
            sweep1[p, at_step(t), :] = got[p]
        return carry

    lax.fori_loop(0, steps, finish, 0, unroll=4)
    for p in range(NP):
        block = sweep1[p].T
        cor_out[2 * p] = block[:stations]
        cor_out[2 * p + 1] = block[stations:]

    for copy in first + halos + second:
        copy.wait_send()


def shards(
    count,
    spaces,
    flow_state,
    forcing,
    pivot_table,
    block_offset,
    line_perm,
    axial_jac,
    radial_jac,
    lower_block,
    upper_block,
):
    _, variables, stations, radial = flow_state.shape
    per = stations // count
    block = jax.ShapeDtypeStruct((variables, stations, radial), f32)
    vmem = pl.BlockSpec(memory_space=pltpu.VMEM)
    dma = pltpu.SemaphoreType.DMA
    exchanged = pltpu.VMEM((count, variables * per, radial), f32)
    residual, correction = pl.pallas_call(
        functools.partial(kernel, count, spaces),
        out_shape=(block, block),
        in_specs=[pl.BlockSpec(memory_space=pltpu.HBM)] * 9,
        out_specs=(vmem, vmem),
        scratch_shapes=[
            pltpu.VMEM((variables, stations, radial), f32),
            pltpu.VMEM((variables, stations, radial), f32),
            pltpu.VMEM((variables, variables, 8, radial), f32),
            pltpu.VMEM((1, stations), jnp.int32),
            pltpu.VMEM((1, radial), jnp.int32),
            pltpu.SMEM((variables, variables), f32),
            pltpu.SMEM((variables, variables), f32),
            pltpu.SMEM((variables, variables), f32),
            pltpu.SMEM((variables, variables), f32),
            dma((9,)),
            pltpu.VMEM((variables, stations + 16, radial), f32),
            pltpu.VMEM((variables, stations, radial), f32),
            exchanged,
            exchanged,
            exchanged,
            exchanged,
            pltpu.VMEM((2, variables, radial), f32),
            pltpu.VMEM((2, variables, radial), f32),
            pltpu.VMEM((896, radial), f32),
            pltpu.VMEM((56, radial, 128), f32),
            pltpu.VMEM((36, radial, 128), f32),
            pltpu.VMEM((4, 256, 256), jnp.bfloat16),
            pltpu.VMEM((NP, radial, 128), f32),
            pltpu.VMEM((NP, radial, 128), f32),
            dma((count - 1,)),
            dma((count - 1,)),
            dma((count - 1,)),
            dma((count - 1,)),
            dma((2,)),
            dma((2,)),
        ],
        compiler_params=pltpu.CompilerParams(
            collective_id=0, has_side_effects=True, vmem_limit_bytes=32 * 1024 * 1024
        ),
    )(
        flow_state[0],
        forcing[0],
        jnp.transpose(pivot_table, (1, 2, 0, 3)),
        block_offset.reshape(1, stations),
        line_perm.reshape(1, radial),
        axial_jac,
        radial_jac,
        lower_block,
        upper_block,
    )
    return residual[None], correction[None]


def solution(mesh):
    spec = P("inst", None, "space", None)
    return jax.shard_map(
        functools.partial(shards, mesh.shape["inst"], mesh.shape["space"]),
        mesh=mesh,
        in_specs=(spec, spec, P(), P("space"), P(), P(), P(), P(), P()),
        out_specs=(spec, spec),
        check_vma=False,
    )
```

```python
import functools

import jax
import jax.numpy as jnp
import numpy as np
from jax import lax
from jax.experimental import pallas as pl
from jax.experimental.pallas import tpu as pltpu
from jax.sharding import PartitionSpec as P

frequency = 0.5
viscosity = 0.01
damping = 0.25

f32 = jnp.float32
MESH = pl.DeviceIdType.MESH
NV = 6
NP = NV // 2
SEG = 8


def spectral_matrix(count):
    index = np.arange(count)
    distance = index[:, None] - index[None, :]
    parity = 1.0 - 2.0 * (distance % 2)
    angle = np.pi * distance / count
    diagonal = distance == 0
    sine = np.where(diagonal, 1.0, np.sin(angle))
    first = np.where(diagonal, 0.0, 0.5 * parity * np.cos(angle) / sine)
    second = np.where(diagonal, -(count * count + 2) / 12.0, -0.5 * parity / (sine * sine))
    return (frequency * first - viscosity * second).astype(np.float32)


def select_columns(x, onehot):
    high = x.astype(jnp.bfloat16)
    rest = x - high.astype(f32)
    middle = rest.astype(jnp.bfloat16)
    low = (rest - middle.astype(f32)).astype(jnp.bfloat16)
    out = jnp.dot(high, onehot, preferred_element_type=f32)
    out = out + jnp.dot(middle, onehot, preferred_element_type=f32)
    return out + jnp.dot(low, onehot, preferred_element_type=f32)


def kernel(
    count,
    spaces,
    state_in,
    forcing_in,
    pivot_in,
    offset_in,
    perm_in,
    ajac_in,
    rjac_in,
    lower_in,
    upper_in,
    res_out,
    cor_out,
    state,
    forcing,
    pivot,
    offset,
    perm,
    ajac,
    rjac,
    lower,
    upper,
    insem,
    line,
    base,
    send1,
    recv1,
    send2,
    recv2,
    halo_out,
    halo_in,
    tab,
    pairc,
    dupc,
    trans,
    jump,
    rhs,
    sweep0,
    sweep1,
    ssem1,
    rsem1,
    ssem2,
    rsem2,
    hssem,
    hrsem,
):
    sources = (
        perm_in, state_in, pivot_in, offset_in, lower_in, upper_in, ajac_in, rjac_in, forcing_in
    )
    targets = (perm, state, pivot, offset, lower, upper, ajac, rjac, forcing)
    loads = [
        pltpu.make_async_copy(source, target, insem.at[i])
        for i, (source, target) in enumerate(zip(sources, targets))
    ]
    for load in loads:
        load.start()
    stations, radial = state.shape[1], state.shape[2]
    per = stations // count
    steps = radial // SEG
    spectral = spectral_matrix(count)
    me = lax.axis_index("inst")
    here = lax.axis_index("space")
    up = lax.rem(here + 1, spaces)
    down = lax.rem(here + spaces - 1, spaces)

    barrier = pltpu.get_barrier_semaphore()
    for d in range(1, count):
        pl.semaphore_signal(
            barrier, inc=1, device_id={"inst": lax.rem(me + d, count)}, device_id_type=MESH
        )
    for other in (up, down):
        pl.semaphore_signal(barrier, inc=1, device_id={"space": other}, device_id_type=MESH)

    loads[0].wait()
    rows = lax.broadcasted_iota(jnp.int32, (radial, radial), 0)
    order = (rows == perm[...]).astype(f32).astype(jnp.bfloat16)
    loads[1].wait()
    flat = select_columns(state[...].reshape(NV * stations, radial), order)
    for v in range(NV):
        block = flat[v * stations : (v + 1) * stations]
        line[v, 8 : 8 + stations, :] = block
        halo_out[0, v : v + 1, :] = block[0:1]
        halo_out[1, v : v + 1, :] = block[stations - 1 : stations]
        for e in range(count):
            send1[e, v * per : (v + 1) * per, :] = block[e * per : (e + 1) * per]

    pl.semaphore_wait(barrier, count + 1)

    def exchange(source, target, ssem, rsem):
        copies = []
        for d in range(count - 1, 0, -1):
            other = lax.rem(me + d, count)
            copies.append(
                pltpu.make_async_remote_copy(
                    src_ref=source.at[other],
                    dst_ref=target.at[me],
                    send_sem=ssem.at[d - 1],
                    recv_sem=rsem.at[d - 1],
                    device_id={"inst": other},
                    device_id_type=MESH,
                )
            )
        return copies

    first = exchange(send1, recv1, ssem1, rsem1)
    for copy in first:
        copy.start()
    halos = []
    for side, other in ((0, down), (1, up)):
        halos.append(
            pltpu.make_async_remote_copy(
                src_ref=halo_out.at[side],
                dst_ref=halo_in.at[side],
                send_sem=hssem.at[side],
                recv_sem=hrsem.at[side],
                device_id={"space": other},
                device_id_type=MESH,
            )
        )
    for copy in halos:
        copy.start()
    recv1[me] = send1[me]

    for load in loads[2:]:
        load.wait()
    for v in range(NV):
        for w in range(NV):
            at = (((v // 2 * NP + w // 2) * 2 + (v % 2 ^ w % 2)) * 2 + v % 2) * 8
            tab[at : at + 8, :] = pivot[v, w]
    tab[288:384, :] = jnp.zeros((96, radial), f32)
    tab[960:, :] = jnp.zeros((64, radial), f32)
    for kind, matrix in ((0, lower), (1, upper)):
        for v in range(NV):
            parts = [pivot[v, u] for u in range(NV)]
            for w in range(NV):
                total = parts[0] * matrix[0, w]
                for u in range(1, NV):
                    total = total + parts[u] * matrix[u, w]
                at = 384 + ((kind * NV + v) * NV + w) * 8
                tab[at : at + 8, :] = -total

    lane = lax.broadcasted_iota(jnp.int32, (256, 256), 1)
    row = lax.broadcasted_iota(jnp.int32, (256, 256), 0) % 128
    wanted = jnp.concatenate([offset[...]] * 4, axis=1)
    for g in range(4):
        hit = row - 32 * g == (lane // 64) * 8 + wanted
        rhs[g] = hit.astype(f32).astype(jnp.bfloat16)
    for g in range(8):
        hit = row - 16 * g == (lane // 128) * 8 + wanted
        rhs[4 + g] = hit.astype(f32).astype(jnp.bfloat16)
    target = lax.broadcasted_iota(jnp.int32, (radial, radial), 0)
    origin = lax.broadcasted_iota(jnp.int32, (radial, radial), 1)
    regroup = (origin == (target % SEG) * steps + target // SEG).astype(f32).astype(jnp.bfloat16)

    def expand(first_block, first_rhs, groups, into):
        def body(b, carry):
            at = pl.multiple_of((first_block + b) * 128, 128)
            block = tab[pl.ds(at, 128), :]
            high = block.astype(jnp.bfloat16)
            low = (block - high.astype(f32)).astype(jnp.bfloat16)
            pieces = jnp.concatenate(
                [
                    lax.dot_general(
                        regroup, x, (((1,), (1,)), ((), ())), preferred_element_type=f32
                    ).astype(jnp.bfloat16)
                    for x in (high, low)
                ],
                axis=1,
            )
            for g in range(groups):
                both = jnp.dot(pieces, rhs[first_rhs + g], preferred_element_type=f32)
                into[(b * groups + g) * 2] = both[:, :128]
                into[(b * groups + g) * 2 + 1] = both[:, 128:]
            return carry

        return body

    lax.fori_loop(0, 3, expand(0, 0, 4, pairc), 0)
    lax.fori_loop(0, 5, expand(3, 4, 8, dupc), 0)

    for copy in first:
        copy.wait_recv()
    for n in range(count):
        total = float(spectral[n, 0]) * recv1[0]
        for m in range(1, count):
            total = total + float(spectral[n, m]) * recv1[m]
        send2[n] = total
    second = exchange(send2, recv2, ssem2, rsem2)
    for copy in second:
        copy.start()
    recv2[me] = send2[me]
    def at_step(t):
        return pl.ds(t, SEG, stride=steps)

    def rows_of(t):
        return pl.ds(pl.multiple_of(t * SEG, SEG), SEG)

    def crossed(pairs):
        return [pltpu.roll(x, 64, 1) for x in pairs]

    def add_up(terms):
        while len(terms) > 1:
            terms = [sum(terms[i : i + 2][1:], terms[i]) for i in range(0, len(terms), 2)]
        return terms[0]

    half = lax.broadcasted_iota(jnp.int32, (SEG, 128), 1) // 64
    segment = lax.broadcasted_iota(jnp.int32, (SEG, 128), 0)

    def spread(pairs):
        turned = crossed(pairs)
        out = []
        for q in range(NP):
            out.append(jnp.where(half == 0, pairs[q], turned[q]))
            out.append(jnp.where(half == 0, turned[q], pairs[q]))
        return out

    def paired(values):
        return [jnp.where(half == 0, values[2 * p], values[2 * p + 1]) for p in range(NP)]

    def load_dup(kind, t):
        return [
            [dupc[(kind * NV + v) * NV + w, rows_of(t), :] for w in range(NV)] for v in range(NV)
        ]

    def shifted(kind, values, by):
        if kind == 0:
            return [jnp.where(segment < by, 0.0, pltpu.roll(x, by, 0)) for x in values]
        return [jnp.where(segment >= SEG - by, 0.0, pltpu.roll(x, SEG - by, 0)) for x in values]

    unit = [
        [jnp.where(2 * q + half == u, 1.0, 0.0).astype(f32) for q in range(NP)] for u in range(NV)
    ]
    for kind in (0, 1):

        def transfer(i, columns):
            t = i if kind == 0 else steps - 1 - i
            coefs = load_dup(kind, t)
            straight = [
                [
                    jnp.where(half == 0, coefs[2 * p][2 * q], coefs[2 * p + 1][2 * q + 1])
                    for q in range(NP)
                ]
                for p in range(NP)
            ]
            cross = [
                [
                    jnp.where(half == 0, coefs[2 * p][2 * q + 1], coefs[2 * p + 1][2 * q])
                    for q in range(NP)
                ]
                for p in range(NP)
            ]
            new = []
            for u in range(NV):
                turned = crossed(columns[u])
                got = []
                for p in range(NP):
                    terms = [straight[p][q] * columns[u][q] for q in range(NP)]
                    terms += [cross[p][q] * turned[q] for q in range(NP)]
                    got.append(add_up(terms))
                    trans[(kind * NV + u) * NP + p, rows_of(t), :] = got[p]
                new.append(got)
            return new

        last = lax.fori_loop(0, steps, transfer, unit, unroll=2)
        over = [shifted(kind, spread(last[u]), 1) for u in range(NV)]
        for level in range(3):
            for u in range(NV):
                for v in range(NV):
                    jump[((kind * 3 + level) * NV + v) * NV + u] = over[u][v]
            if level < 2:
                before = [shifted(kind, over[u], 1 << level) for u in range(NV)]
                over = [
                    [
                        add_up([over[w][v] * before[u][w] for w in range(NV)])
                        for v in range(NV)
                    ]
                    for u in range(NV)
                ]

    order_forcing = select_columns(forcing[...].reshape(NV * stations, radial), order)
    for copy in halos:
        copy.wait_recv()
    for v in range(NV):
        line[v, 8 + stations : 9 + stations, :] = jnp.where(
            here == spaces - 1, 0.0, halo_in[0, v : v + 1, :]
        )
        line[v, 7:8, :] = jnp.where(here == 0, 0.0, halo_in[1, v : v + 1, :])

    spot = lax.broadcasted_iota(jnp.int32, (8, radial), 1)

    def local(i, carry):
        at = pl.multiple_of(i * 8, 8)
        axial, outward, mean = [], [], []
        for v in range(NV):
            window = line[v, pl.ds(at, 24), :]
            centre = window[8:16]
            ahead = window[9:17]
            behind = window[7:15]
            outer = jnp.where(spot == radial - 1, 0.0, pltpu.roll(centre, radial - 1, 1))
            inner = jnp.where(spot == 0, 0.0, pltpu.roll(centre, 1, 1))
            axial.append(0.5 * (ahead - behind))
            outward.append(0.5 * (outer - inner))
            mean.append(damping * (ahead + behind + outer + inner - 4.0 * centre))
        for v in range(NV):
            total = ajac[v, 0] * axial[0] + rjac[v, 0] * outward[0]
            for w in range(1, NV):
                total = total + (ajac[v, w] * axial[w] + rjac[v, w] * outward[w])
            base[v, pl.ds(at, 8), :] = total - mean[v]
        return carry

    lax.fori_loop(0, stations // 8, local, 0)
    for v in range(NV):
        base[v] = base[v] - order_forcing[v * stations : (v + 1) * stations]

    for copy in second:
        copy.wait_recv()

    pairs = []
    for p in range(NP):
        blocks = []
        for v in (2 * p, 2 * p + 1):
            timed = jnp.concatenate(
                [recv2[e, v * per : (v + 1) * per, :] for e in range(count)], axis=0
            )
            residual = base[v] + timed
            res_out[v] = residual
            blocks.append(residual)
        sweep0[p] = jnp.concatenate(blocks, axis=0).T

    zeros = [jnp.zeros((SEG, 128), f32) for _ in range(NV)]

    def add_transfer(kind, t, start, entering):
        return [
            add_up(
                [start[p]]
                + [
                    trans[(kind * NV + u) * NP + p, rows_of(t), :] * entering[u]
                    for u in range(NV)
                ]
            )
            for p in range(NP)
        ]

    def advance(coefs, held, start):
        return [
            add_up([coefs[v][w] * held[w] for w in range(NV)]) + start[v] for v in range(NV)
        ]

    def carries(kind, ends):
        held = shifted(kind, ends, 1)
        for level in range(3):
            base_at = (kind * 3 + level) * NV * NV
            coefs = [[jump[base_at + v * NV + u] for u in range(NV)] for v in range(NV)]
            held = advance(coefs, shifted(kind, held, 1 << level), held)
        return held

    def forward(t, held):
        source = [sweep0[p, at_step(t), :] for p in range(NP)]
        turned = crossed(source)
        start = []
        for p in range(NP):
            terms = []
            for q in range(NP):
                at = (p * NP + q) * 2
                terms.append(pairc[at, rows_of(t), :] * source[q])
                terms.append(pairc[at + 1, rows_of(t), :] * turned[q])
            start.append(add_up(terms))
        got = advance(load_dup(0, t), held, spread(start))
        for p, x in enumerate(paired(got)):
            sweep1[p, rows_of(t), :] = x
        return got

    ends = lax.fori_loop(0, steps, forward, zeros, unroll=True)
    entering = carries(0, ends)

    def backward(i, held):
        t = steps - 1 - i
        start = add_transfer(0, t, [sweep1[p, rows_of(t), :] for p in range(NP)], entering)
        got = advance(load_dup(1, t), held, spread(start))
        for p, x in enumerate(paired(got)):
            sweep0[p, rows_of(t), :] = x
        return got

    ends = lax.fori_loop(0, steps, backward, zeros, unroll=True)
    leaving = carries(1, ends)

    def finish(t, carry):
        got = add_transfer(1, t, [sweep0[p, rows_of(t), :] for p in range(NP)], leaving)
        for p in range(NP):
            sweep1[p, at_step(t), :] = got[p]
        return carry

    lax.fori_loop(0, steps, finish, 0, unroll=4)
    for p in range(NP):
        block = sweep1[p].T
        cor_out[2 * p] = block[:stations]
        cor_out[2 * p + 1] = block[stations:]

    for copy in first + halos + second:
        copy.wait_send()


def shards(
    count,
    spaces,
    flow_state,
    forcing,
    pivot_table,
    block_offset,
    line_perm,
    axial_jac,
    radial_jac,
    lower_block,
    upper_block,
):
    _, variables, stations, radial = flow_state.shape
    per = stations // count
    block = jax.ShapeDtypeStruct((variables, stations, radial), f32)
    vmem = pl.BlockSpec(memory_space=pltpu.VMEM)
    dma = pltpu.SemaphoreType.DMA
    exchanged = pltpu.VMEM((count, variables * per, radial), f32)
    residual, correction = pl.pallas_call(
        functools.partial(kernel, count, spaces),
        out_shape=(block, block),
        in_specs=[pl.BlockSpec(memory_space=pltpu.HBM)] * 9,
        out_specs=(vmem, vmem),
        scratch_shapes=[
            pltpu.VMEM((variables, stations, radial), f32),
            pltpu.VMEM((variables, stations, radial), f32),
            pltpu.VMEM((variables, variables, 8, radial), f32),
            pltpu.VMEM((1, stations), jnp.int32),
            pltpu.VMEM((1, radial), jnp.int32),
            pltpu.SMEM((variables, variables), f32),
            pltpu.SMEM((variables, variables), f32),
            pltpu.SMEM((variables, variables), f32),
            pltpu.SMEM((variables, variables), f32),
            dma((9,)),
            pltpu.VMEM((variables, stations + 16, radial), f32),
            pltpu.VMEM((variables, stations, radial), f32),
            exchanged,
            exchanged,
            exchanged,
            exchanged,
            pltpu.VMEM((2, variables, radial), f32),
            pltpu.VMEM((2, variables, radial), f32),
            pltpu.VMEM((1024, radial), f32),
            pltpu.VMEM((24, radial, 128), f32),
            pltpu.VMEM((80, radial, 128), f32),
            pltpu.VMEM((36, radial, 128), f32),
            pltpu.VMEM((6 * variables * variables, SEG, 128), f32),
            pltpu.VMEM((12, 256, 256), jnp.bfloat16),
            pltpu.VMEM((NP, radial, 128), f32),
            pltpu.VMEM((NP, radial, 128), f32),
            dma((count - 1,)),
            dma((count - 1,)),
            dma((count - 1,)),
            dma((count - 1,)),
            dma((2,)),
            dma((2,)),
        ],
        compiler_params=pltpu.CompilerParams(
            collective_id=0, has_side_effects=True, vmem_limit_bytes=32 * 1024 * 1024
        ),
    )(
        *(
            pltpu.with_memory_space_constraint(x, pltpu.HBM)
            for x in (
                flow_state[0],
                forcing[0],
                jnp.transpose(pivot_table, (1, 2, 0, 3)),
                block_offset.reshape(1, stations),
                line_perm.reshape(1, radial),
                axial_jac,
                radial_jac,
                lower_block,
                upper_block,
            )
        )
    )
    return residual[None], correction[None]


def solution(mesh):
    spec = P("inst", None, "space", None)
    return jax.shard_map(
        functools.partial(shards, mesh.shape["inst"], mesh.shape["space"]),
        mesh=mesh,
        in_specs=(spec, spec, P(), P("space"), P(), P(), P(), P(), P()),
        out_specs=(spec, spec),
        check_vma=False,
    )
```

```python
import functools

import jax
import jax.numpy as jnp
import numpy as np
from jax import lax
from jax.experimental import pallas as pl
from jax.experimental.pallas import tpu as pltpu
from jax.sharding import PartitionSpec as P

frequency = 0.5
viscosity = 0.01
damping = 0.25

f32 = jnp.float32
MESH = pl.DeviceIdType.MESH
NV = 6
NP = NV // 2
SEG = 8


def spectral_matrix(count):
    index = np.arange(count)
    distance = index[:, None] - index[None, :]
    parity = 1.0 - 2.0 * (distance % 2)
    angle = np.pi * distance / count
    diagonal = distance == 0
    sine = np.where(diagonal, 1.0, np.sin(angle))
    first = np.where(diagonal, 0.0, 0.5 * parity * np.cos(angle) / sine)
    second = np.where(diagonal, -(count * count + 2) / 12.0, -0.5 * parity / (sine * sine))
    return (frequency * first - viscosity * second).astype(np.float32)


def select_columns(x, onehot):
    high = x.astype(jnp.bfloat16)
    rest = x - high.astype(f32)
    middle = rest.astype(jnp.bfloat16)
    low = (rest - middle.astype(f32)).astype(jnp.bfloat16)
    out = jnp.dot(high, onehot, preferred_element_type=f32)
    out = out + jnp.dot(middle, onehot, preferred_element_type=f32)
    return out + jnp.dot(low, onehot, preferred_element_type=f32)


def kernel(
    count,
    spaces,
    state_in,
    forcing_in,
    pivot_in,
    offset_in,
    perm_in,
    ajac_in,
    rjac_in,
    lower_in,
    upper_in,
    res_out,
    cor_out,
    state,
    forcing,
    pivot,
    offset,
    perm,
    ajac,
    rjac,
    lower,
    upper,
    insem,
    line,
    base,
    send1,
    recv1,
    send2,
    recv2,
    halo_out,
    halo_in,
    tab,
    pairc,
    dupc,
    trans,
    jump,
    rhs,
    pieces,
    sweep0,
    sweep1,
    ssem1,
    rsem1,
    ssem2,
    rsem2,
    hssem,
    hrsem,
):
    sources = (
        perm_in, state_in, pivot_in, offset_in, lower_in, upper_in, ajac_in, rjac_in, forcing_in
    )
    targets = (perm, state, pivot, offset, lower, upper, ajac, rjac, forcing)
    loads = [
        pltpu.make_async_copy(source, target, insem.at[i])
        for i, (source, target) in enumerate(zip(sources, targets))
    ]
    for load in loads:
        load.start()
    stations, radial = state.shape[1], state.shape[2]
    per = stations // count
    steps = radial // SEG
    spectral = spectral_matrix(count)
    me = lax.axis_index("inst")
    here = lax.axis_index("space")
    up = lax.rem(here + 1, spaces)
    down = lax.rem(here + spaces - 1, spaces)

    barrier = pltpu.get_barrier_semaphore()
    for d in range(1, count):
        pl.semaphore_signal(
            barrier, inc=1, device_id={"inst": lax.rem(me + d, count)}, device_id_type=MESH
        )
    for other in (up, down):
        pl.semaphore_signal(barrier, inc=1, device_id={"space": other}, device_id_type=MESH)

    loads[0].wait()
    rows = lax.broadcasted_iota(jnp.int32, (radial, radial), 0)
    order = (rows == perm[...]).astype(f32).astype(jnp.bfloat16)
    loads[1].wait()
    flat = select_columns(state[...].reshape(NV * stations, radial), order)
    for v in range(NV):
        block = flat[v * stations : (v + 1) * stations]
        line[v, 8 : 8 + stations, :] = block
        halo_out[0, v : v + 1, :] = block[0:1]
        halo_out[1, v : v + 1, :] = block[stations - 1 : stations]
        for e in range(count):
            send1[e, v * per : (v + 1) * per, :] = block[e * per : (e + 1) * per]

    pl.semaphore_wait(barrier, count + 1)

    def exchange(source, target, ssem, rsem):
        copies = []
        for d in range(count - 1, 0, -1):
            other = lax.rem(me + d, count)
            copies.append(
                pltpu.make_async_remote_copy(
                    src_ref=source.at[other],
                    dst_ref=target.at[me],
                    send_sem=ssem.at[d - 1],
                    recv_sem=rsem.at[d - 1],
                    device_id={"inst": other},
                    device_id_type=MESH,
                )
            )
        return copies

    first = exchange(send1, recv1, ssem1, rsem1)
    for copy in first:
        copy.start()
    halos = []
    for side, other in ((0, down), (1, up)):
        halos.append(
            pltpu.make_async_remote_copy(
                src_ref=halo_out.at[side],
                dst_ref=halo_in.at[side],
                send_sem=hssem.at[side],
                recv_sem=hrsem.at[side],
                device_id={"space": other},
                device_id_type=MESH,
            )
        )
    for copy in halos:
        copy.start()
    recv1[me] = send1[me]

    for load in loads[2:]:
        load.wait()
    for v in range(NV):
        for w in range(NV):
            at = (((v // 2 * NP + w // 2) * 2 + (v % 2 ^ w % 2)) * 2 + v % 2) * 8
            tab[at : at + 8, :] = pivot[v, w]
    tab[288:384, :] = jnp.zeros((96, radial), f32)
    tab[960:, :] = jnp.zeros((64, radial), f32)
    for kind, matrix in ((0, lower), (1, upper)):
        for v in range(NV):
            parts = [pivot[v, u] for u in range(NV)]
            for w in range(NV):
                total = parts[0] * matrix[0, w]
                for u in range(1, NV):
                    total = total + parts[u] * matrix[u, w]
                at = 384 + ((kind * NV + v) * NV + w) * 8
                tab[at : at + 8, :] = -total

    lane = lax.broadcasted_iota(jnp.int32, (32, 256), 1)
    row = lax.broadcasted_iota(jnp.int32, (32, 256), 0)
    wanted = jnp.concatenate([offset[...]] * 4, axis=1)
    rhs[...] = jnp.zeros_like(rhs)
    hit = (row == (lane // 64) * 8 + wanted).astype(f32).astype(jnp.bfloat16)
    for g in range(4):
        for piece in (0, 128):
            rhs[g, piece + 32 * g : piece + 32 * g + 32, :] = hit
    hit = (row == (lane // 128) * 8 + wanted)[:16].astype(f32).astype(jnp.bfloat16)
    for g in range(8):
        for piece in (0, 128):
            rhs[4 + g, piece + 16 * g : piece + 16 * g + 16, :] = hit
    target = lax.broadcasted_iota(jnp.int32, (radial, radial), 0)
    origin = lax.broadcasted_iota(jnp.int32, (radial, radial), 1)
    regroup = (origin == (target % SEG) * steps + target // SEG).astype(f32).astype(jnp.bfloat16)

    def split(b, carry):
        at = pl.multiple_of(b * 128, 128)
        block = tab[pl.ds(at, 128), :]
        high = block.astype(jnp.bfloat16)
        low = (block - high.astype(f32)).astype(jnp.bfloat16)
        for i, x in enumerate((high, low)):
            pieces[pl.ds(at, 128), i * 128 : i * 128 + 128] = lax.dot_general(
                regroup, x, (((1,), (1,)), ((), ())), preferred_element_type=f32
            ).astype(jnp.bfloat16)
        return carry

    lax.fori_loop(0, 8, split, 0, unroll=2)

    def expand(first_block, blocks, first_rhs, groups, into):
        def body(g, carry):
            both = jnp.dot(
                pieces[first_block * 128 : (first_block + blocks) * 128, :],
                rhs[first_rhs + g],
                preferred_element_type=f32,
            )
            for b in range(blocks):
                into[(b * groups + g) * 2] = both[b * 128 : b * 128 + 128, :128]
                into[(b * groups + g) * 2 + 1] = both[b * 128 : b * 128 + 128, 128:]
            return carry

        lax.fori_loop(0, groups, body, 0)

    expand(0, 3, 0, 4, pairc)
    expand(3, 5, 4, 8, dupc)

    for copy in first:
        copy.wait_recv()
    for n in range(count):
        total = float(spectral[n, 0]) * recv1[0]
        for m in range(1, count):
            total = total + float(spectral[n, m]) * recv1[m]
        send2[n] = total
    second = exchange(send2, recv2, ssem2, rsem2)
    for copy in second:
        copy.start()
    recv2[me] = send2[me]
    def at_step(t):
        return pl.ds(t, SEG, stride=steps)

    def rows_of(t):
        return pl.ds(pl.multiple_of(t * SEG, SEG), SEG)

    def crossed(pairs):
        return [pltpu.roll(x, 64, 1) for x in pairs]

    def add_up(terms):
        while len(terms) > 1:
            terms = [sum(terms[i : i + 2][1:], terms[i]) for i in range(0, len(terms), 2)]
        return terms[0]

    half = lax.broadcasted_iota(jnp.int32, (SEG, 128), 1) // 64
    segment = lax.broadcasted_iota(jnp.int32, (SEG, 128), 0)

    def spread(pairs):
        turned = crossed(pairs)
        out = []
        for q in range(NP):
            out.append(jnp.where(half == 0, pairs[q], turned[q]))
            out.append(jnp.where(half == 0, turned[q], pairs[q]))
        return out

    def paired(values):
        return [jnp.where(half == 0, values[2 * p], values[2 * p + 1]) for p in range(NP)]

    def load_dup(kind, t):
        return [
            [dupc[(kind * NV + v) * NV + w, rows_of(t), :] for w in range(NV)] for v in range(NV)
        ]

    def shifted(kind, values, by):
        if kind == 0:
            return [jnp.where(segment < by, 0.0, pltpu.roll(x, by, 0)) for x in values]
        return [jnp.where(segment >= SEG - by, 0.0, pltpu.roll(x, SEG - by, 0)) for x in values]

    unit = [
        [jnp.where(2 * q + half == u, 1.0, 0.0).astype(f32) for q in range(NP)] for u in range(NV)
    ]
    for kind in (0, 1):

        def transfer(i, columns):
            t = i if kind == 0 else steps - 1 - i
            coefs = load_dup(kind, t)
            straight = [
                [
                    jnp.where(half == 0, coefs[2 * p][2 * q], coefs[2 * p + 1][2 * q + 1])
                    for q in range(NP)
                ]
                for p in range(NP)
            ]
            cross = [
                [
                    jnp.where(half == 0, coefs[2 * p][2 * q + 1], coefs[2 * p + 1][2 * q])
                    for q in range(NP)
                ]
                for p in range(NP)
            ]
            new = []
            for u in range(NV):
                turned = crossed(columns[u])
                got = []
                for p in range(NP):
                    terms = [straight[p][q] * columns[u][q] for q in range(NP)]
                    terms += [cross[p][q] * turned[q] for q in range(NP)]
                    got.append(add_up(terms))
                    trans[(kind * NV + u) * NP + p, rows_of(t), :] = got[p]
                new.append(got)
            return new

        last = lax.fori_loop(0, steps, transfer, unit, unroll=2)
        over = [shifted(kind, spread(last[u]), 1) for u in range(NV)]
        for level in range(3):
            for u in range(NV):
                for v in range(NV):
                    jump[((kind * 3 + level) * NV + v) * NV + u] = over[u][v]
            if level < 2:
                before = [shifted(kind, over[u], 1 << level) for u in range(NV)]
                over = [
                    [
                        add_up([over[w][v] * before[u][w] for w in range(NV)])
                        for v in range(NV)
                    ]
                    for u in range(NV)
                ]

    order_forcing = select_columns(forcing[...].reshape(NV * stations, radial), order)
    for copy in halos:
        copy.wait_recv()
    for v in range(NV):
        line[v, 8 + stations : 9 + stations, :] = jnp.where(
            here == spaces - 1, 0.0, halo_in[0, v : v + 1, :]
        )
        line[v, 7:8, :] = jnp.where(here == 0, 0.0, halo_in[1, v : v + 1, :])

    spot = lax.broadcasted_iota(jnp.int32, (8, radial), 1)

    def local(i, carry):
        at = pl.multiple_of(i * 8, 8)
        axial, outward, mean = [], [], []
        for v in range(NV):
            window = line[v, pl.ds(at, 24), :]
            centre = window[8:16]
            ahead = window[9:17]
            behind = window[7:15]
            outer = jnp.where(spot == radial - 1, 0.0, pltpu.roll(centre, radial - 1, 1))
            inner = jnp.where(spot == 0, 0.0, pltpu.roll(centre, 1, 1))
            axial.append(0.5 * (ahead - behind))
            outward.append(0.5 * (outer - inner))
            mean.append(damping * (ahead + behind + outer + inner - 4.0 * centre))
        for v in range(NV):
            total = ajac[v, 0] * axial[0] + rjac[v, 0] * outward[0]
            for w in range(1, NV):
                total = total + (ajac[v, w] * axial[w] + rjac[v, w] * outward[w])
            base[v, pl.ds(at, 8), :] = total - mean[v]
        return carry

    lax.fori_loop(0, stations // 8, local, 0)
    for v in range(NV):
        base[v] = base[v] - order_forcing[v * stations : (v + 1) * stations]

    for copy in second:
        copy.wait_recv()

    pairs = []
    for p in range(NP):
        blocks = []
        for v in (2 * p, 2 * p + 1):
            timed = jnp.concatenate(
                [recv2[e, v * per : (v + 1) * per, :] for e in range(count)], axis=0
            )
            residual = base[v] + timed
            res_out[v] = residual
            blocks.append(residual)
        sweep0[p] = jnp.concatenate(blocks, axis=0).T

    zeros = [jnp.zeros((SEG, 128), f32) for _ in range(NV)]

    def add_transfer(kind, t, start, entering):
        return [
            add_up(
                [start[p]]
                + [
                    trans[(kind * NV + u) * NP + p, rows_of(t), :] * entering[u]
                    for u in range(NV)
                ]
            )
            for p in range(NP)
        ]

    def advance(coefs, held, start):
        return [
            add_up([coefs[v][w] * held[w] for w in range(NV)]) + start[v] for v in range(NV)
        ]

    def carries(kind, ends):
        held = shifted(kind, ends, 1)
        for level in range(3):
            base_at = (kind * 3 + level) * NV * NV
            coefs = [[jump[base_at + v * NV + u] for u in range(NV)] for v in range(NV)]
            held = advance(coefs, shifted(kind, held, 1 << level), held)
        return held

    def forward(t, held):
        source = [sweep0[p, at_step(t), :] for p in range(NP)]
        turned = crossed(source)
        start = []
        for p in range(NP):
            terms = []
            for q in range(NP):
                at = (p * NP + q) * 2
                terms.append(pairc[at, rows_of(t), :] * source[q])
                terms.append(pairc[at + 1, rows_of(t), :] * turned[q])
            start.append(add_up(terms))
        got = advance(load_dup(0, t), held, spread(start))
        for p, x in enumerate(paired(got)):
            sweep1[p, rows_of(t), :] = x
        return got

    ends = lax.fori_loop(0, steps, forward, zeros, unroll=True)
    entering = carries(0, ends)

    def backward(i, held):
        t = steps - 1 - i
        start = add_transfer(0, t, [sweep1[p, rows_of(t), :] for p in range(NP)], entering)
        got = advance(load_dup(1, t), held, spread(start))
        for p, x in enumerate(paired(got)):
            sweep0[p, rows_of(t), :] = x
        return got

    ends = lax.fori_loop(0, steps, backward, zeros, unroll=True)
    leaving = carries(1, ends)

    def finish(t, carry):
        got = add_transfer(1, t, [sweep0[p, rows_of(t), :] for p in range(NP)], leaving)
        for p in range(NP):
            sweep1[p, at_step(t), :] = got[p]
        return carry

    lax.fori_loop(0, steps, finish, 0, unroll=4)
    for p in range(NP):
        block = sweep1[p].T
        cor_out[2 * p] = block[:stations]
        cor_out[2 * p + 1] = block[stations:]

    for copy in first + halos + second:
        copy.wait_send()


def deliver(residual, correction, res_out, cor_out, sem):
    copies = [
        pltpu.make_async_copy(residual, res_out, sem.at[0]),
        pltpu.make_async_copy(correction, cor_out, sem.at[1]),
    ]
    for copy in copies:
        copy.start()
    for copy in copies:
        copy.wait()


def shards(
    count,
    spaces,
    flow_state,
    forcing,
    pivot_table,
    block_offset,
    line_perm,
    axial_jac,
    radial_jac,
    lower_block,
    upper_block,
):
    _, variables, stations, radial = flow_state.shape
    per = stations // count
    block = jax.ShapeDtypeStruct((variables, stations, radial), f32)
    vmem = pl.BlockSpec(memory_space=pltpu.VMEM)
    dma = pltpu.SemaphoreType.DMA
    exchanged = pltpu.VMEM((count, variables * per, radial), f32)
    residual, correction = pl.pallas_call(
        functools.partial(kernel, count, spaces),
        out_shape=(block, block),
        in_specs=[pl.BlockSpec(memory_space=pltpu.HBM)] * 9,
        out_specs=(vmem, vmem),
        scratch_shapes=[
            pltpu.VMEM((variables, stations, radial), f32),
            pltpu.VMEM((variables, stations, radial), f32),
            pltpu.VMEM((variables, variables, 8, radial), f32),
            pltpu.VMEM((1, stations), jnp.int32),
            pltpu.VMEM((1, radial), jnp.int32),
            pltpu.SMEM((variables, variables), f32),
            pltpu.SMEM((variables, variables), f32),
            pltpu.SMEM((variables, variables), f32),
            pltpu.SMEM((variables, variables), f32),
            dma((9,)),
            pltpu.VMEM((variables, stations + 16, radial), f32),
            pltpu.VMEM((variables, stations, radial), f32),
            exchanged,
            exchanged,
            exchanged,
            exchanged,
            pltpu.VMEM((2, variables, radial), f32),
            pltpu.VMEM((2, variables, radial), f32),
            pltpu.VMEM((1024, radial), f32),
            pltpu.VMEM((24, radial, 128), f32),
            pltpu.VMEM((80, radial, 128), f32),
            pltpu.VMEM((36, radial, 128), f32),
            pltpu.VMEM((6 * variables * variables, SEG, 128), f32),
            pltpu.VMEM((12, 256, 256), jnp.bfloat16),
            pltpu.VMEM((1024, 256), jnp.bfloat16),
            pltpu.VMEM((NP, radial, 128), f32),
            pltpu.VMEM((NP, radial, 128), f32),
            dma((count - 1,)),
            dma((count - 1,)),
            dma((count - 1,)),
            dma((count - 1,)),
            dma((2,)),
            dma((2,)),
        ],
        compiler_params=pltpu.CompilerParams(
            collective_id=0, has_side_effects=True, vmem_limit_bytes=32 * 1024 * 1024
        ),
    )(
        *(
            pltpu.with_memory_space_constraint(x, pltpu.HBM)
            for x in (
                flow_state[0],
                forcing[0],
                jnp.transpose(pivot_table, (1, 2, 0, 3)),
                block_offset.reshape(1, stations),
                line_perm.reshape(1, radial),
                axial_jac,
                radial_jac,
                lower_block,
                upper_block,
            )
        )
    )
    anywhere = pl.BlockSpec(memory_space=pl.ANY)
    residual, correction = pl.pallas_call(
        deliver,
        out_shape=(block, block),
        in_specs=[anywhere] * 2,
        out_specs=(anywhere, anywhere),
        scratch_shapes=[dma((2,))],
    )(residual, correction)
    return residual[None], correction[None]


def solution(mesh):
    spec = P("inst", None, "space", None)
    return jax.shard_map(
        functools.partial(shards, mesh.shape["inst"], mesh.shape["space"]),
        mesh=mesh,
        in_specs=(spec, spec, P(), P("space"), P(), P(), P(), P(), P()),
        out_specs=(spec, spec),
        check_vma=False,
    )
```

```python
import functools

import jax
import jax.numpy as jnp
import numpy as np
from jax import lax
from jax.experimental import pallas as pl
from jax.experimental.pallas import tpu as pltpu
from jax.sharding import PartitionSpec as P

frequency = 0.5
viscosity = 0.01
damping = 0.25

f32 = jnp.float32
MESH = pl.DeviceIdType.MESH
NV = 6
NP = NV // 2
SEG = 8


def spectral_matrix(count):
    index = np.arange(count)
    distance = index[:, None] - index[None, :]
    parity = 1.0 - 2.0 * (distance % 2)
    angle = np.pi * distance / count
    diagonal = distance == 0
    sine = np.where(diagonal, 1.0, np.sin(angle))
    first = np.where(diagonal, 0.0, 0.5 * parity * np.cos(angle) / sine)
    second = np.where(diagonal, -(count * count + 2) / 12.0, -0.5 * parity / (sine * sine))
    return (frequency * first - viscosity * second).astype(np.float32)


def select_columns(x, onehot):
    high = x.astype(jnp.bfloat16)
    rest = x - high.astype(f32)
    middle = rest.astype(jnp.bfloat16)
    low = (rest - middle.astype(f32)).astype(jnp.bfloat16)
    out = jnp.dot(high, onehot, preferred_element_type=f32)
    out = out + jnp.dot(middle, onehot, preferred_element_type=f32)
    return out + jnp.dot(low, onehot, preferred_element_type=f32)


def kernel(
    count,
    spaces,
    state_in,
    forcing_in,
    pivot_in,
    offset_in,
    perm_in,
    ajac_in,
    rjac_in,
    lower_in,
    upper_in,
    res_out,
    cor_out,
    state,
    forcing,
    pivot,
    offset,
    perm,
    ajac,
    rjac,
    lower,
    upper,
    insem,
    line,
    base,
    send1,
    recv1,
    send2,
    recv2,
    halo_out,
    halo_in,
    tab,
    pairc,
    dupc,
    trans,
    jump,
    rhs,
    pieces,
    sweep0,
    sweep1,
    ssem1,
    rsem1,
    ssem2,
    rsem2,
    hssem,
    hrsem,
    go,
):
    sources = (
        perm_in, state_in, pivot_in, offset_in, lower_in, upper_in, ajac_in, rjac_in, forcing_in
    )
    targets = (perm, state, pivot, offset, lower, upper, ajac, rjac, forcing)
    loads = [
        pltpu.make_async_copy(source, target, insem.at[i])
        for i, (source, target) in enumerate(zip(sources, targets))
    ]
    for load in loads:
        load.start()
    stations, radial = state.shape[1], state.shape[2]
    per = stations // count
    steps = radial // SEG
    spectral = spectral_matrix(count)
    me = lax.axis_index("inst")
    here = lax.axis_index("space")
    up = lax.rem(here + 1, spaces)
    down = lax.rem(here + spaces - 1, spaces)

    barrier = pltpu.get_barrier_semaphore()
    gate, informer = count - 1, count - 2
    for n in range(gate):

        @pl.when(me != n)
        def _():
            pl.semaphore_signal(barrier, inc=1, device_id={"inst": n}, device_id_type=MESH)

    for other in (up, down):
        pl.semaphore_signal(
            barrier, inc=1, device_id={"inst": gate, "space": other}, device_id_type=MESH
        )

    loads[0].wait()
    rows = lax.broadcasted_iota(jnp.int32, (radial, radial), 0)
    order = (rows == perm[...]).astype(f32).astype(jnp.bfloat16)
    loads[1].wait()
    flat = select_columns(state[...].reshape(NV * stations, radial), order)
    for v in range(NV):
        block = flat[v * stations : (v + 1) * stations]
        line[v, 8 : 8 + stations, :] = block
        halo_out[0, v : v + 1, :] = block[0:1]
        halo_out[1, v : v + 1, :] = block[stations - 1 : stations]
        for e in range(count):
            send1[e, v * per : (v + 1) * per, :] = block[e * per : (e + 1) * per]

    @pl.when(me != gate)
    def _():
        pl.semaphore_wait(barrier, count - 1)

    @pl.when(me == informer)
    def _():
        pl.semaphore_signal(go, inc=1, device_id={"inst": gate}, device_id_type=MESH)

    @pl.when(me == gate)
    def _():
        pl.semaphore_wait(go, 1)

    def exchange(source, target, ssem, rsem):
        copies = []
        for d in range(count - 1, 0, -1):
            other = lax.rem(me + d, count)
            copies.append(
                pltpu.make_async_remote_copy(
                    src_ref=source.at[other],
                    dst_ref=target.at[me],
                    send_sem=ssem.at[d - 1],
                    recv_sem=rsem.at[d - 1],
                    device_id={"inst": other},
                    device_id_type=MESH,
                )
            )
        return copies

    first = exchange(send1, recv1, ssem1, rsem1)
    for copy in first:
        copy.start()
    halos = []
    for side, other in ((0, down), (1, up)):
        halos.append(
            pltpu.make_async_remote_copy(
                src_ref=halo_out.at[side],
                dst_ref=halo_in.at[side],
                send_sem=hssem.at[side],
                recv_sem=hrsem.at[side],
                device_id={"space": other},
                device_id_type=MESH,
            )
        )
    recv1[me] = send1[me]

    for load in loads[2:]:
        load.wait()
    for v in range(NV):
        for w in range(NV):
            at = (((v // 2 * NP + w // 2) * 2 + (v % 2 ^ w % 2)) * 2 + v % 2) * 8
            tab[at : at + 8, :] = pivot[v, w]
    tab[288:384, :] = jnp.zeros((96, radial), f32)
    tab[960:, :] = jnp.zeros((64, radial), f32)
    for kind, matrix in ((0, lower), (1, upper)):
        for v in range(NV):
            parts = [pivot[v, u] for u in range(NV)]
            for w in range(NV):
                total = parts[0] * matrix[0, w]
                for u in range(1, NV):
                    total = total + parts[u] * matrix[u, w]
                at = 384 + ((kind * NV + v) * NV + w) * 8
                tab[at : at + 8, :] = -total

    lane = lax.broadcasted_iota(jnp.int32, (32, 256), 1)
    row = lax.broadcasted_iota(jnp.int32, (32, 256), 0)
    wanted = jnp.concatenate([offset[...]] * 4, axis=1)
    rhs[...] = jnp.zeros_like(rhs)
    hit = (row == (lane // 64) * 8 + wanted).astype(f32).astype(jnp.bfloat16)
    for g in range(4):
        for piece in (0, 128):
            rhs[g, piece + 32 * g : piece + 32 * g + 32, :] = hit
    hit = (row == (lane // 128) * 8 + wanted)[:16].astype(f32).astype(jnp.bfloat16)
    for g in range(8):
        for piece in (0, 128):
            rhs[4 + g, piece + 16 * g : piece + 16 * g + 16, :] = hit
    target = lax.broadcasted_iota(jnp.int32, (radial, radial), 0)
    origin = lax.broadcasted_iota(jnp.int32, (radial, radial), 1)
    regroup = (origin == (target % SEG) * steps + target // SEG).astype(f32).astype(jnp.bfloat16)

    def split(b, carry):
        at = pl.multiple_of(b * 128, 128)
        block = tab[pl.ds(at, 128), :]
        high = block.astype(jnp.bfloat16)
        low = (block - high.astype(f32)).astype(jnp.bfloat16)
        for i, x in enumerate((high, low)):
            pieces[pl.ds(at, 128), i * 128 : i * 128 + 128] = lax.dot_general(
                regroup, x, (((1,), (1,)), ((), ())), preferred_element_type=f32
            ).astype(jnp.bfloat16)
        return carry

    lax.fori_loop(0, 8, split, 0, unroll=2)

    def expand(first_block, blocks, first_rhs, groups, into):
        def body(g, carry):
            both = jnp.dot(
                pieces[first_block * 128 : (first_block + blocks) * 128, :],
                rhs[first_rhs + g],
                preferred_element_type=f32,
            )
            for b in range(blocks):
                into[(b * groups + g) * 2] = both[b * 128 : b * 128 + 128, :128]
                into[(b * groups + g) * 2 + 1] = both[b * 128 : b * 128 + 128, 128:]
            return carry

        lax.fori_loop(0, groups, body, 0)

    expand(0, 3, 0, 4, pairc)
    expand(3, 5, 4, 8, dupc)

    @pl.when(me == gate)
    def _():
        pl.semaphore_wait(barrier, 2 * count)
        for n in range(gate):
            pl.semaphore_signal(go, inc=1, device_id={"inst": n}, device_id_type=MESH)

    for copy in first:
        copy.wait_recv()
    for n in range(count):
        total = float(spectral[n, 0]) * recv1[0]
        for m in range(1, count):
            total = total + float(spectral[n, m]) * recv1[m]
        send2[n] = total
    second = exchange(send2, recv2, ssem2, rsem2)
    for copy in second:
        copy.start()
    recv2[me] = send2[me]

    @pl.when(me != gate)
    def _():
        pl.semaphore_wait(go, 1)

    for copy in halos:
        copy.start()

    def at_step(t):
        return pl.ds(t, SEG, stride=steps)

    def rows_of(t):
        return pl.ds(pl.multiple_of(t * SEG, SEG), SEG)

    def crossed(pairs):
        return [pltpu.roll(x, 64, 1) for x in pairs]

    def add_up(terms):
        while len(terms) > 1:
            terms = [sum(terms[i : i + 2][1:], terms[i]) for i in range(0, len(terms), 2)]
        return terms[0]

    half = lax.broadcasted_iota(jnp.int32, (SEG, 128), 1) // 64
    segment = lax.broadcasted_iota(jnp.int32, (SEG, 128), 0)

    def spread(pairs):
        turned = crossed(pairs)
        out = []
        for q in range(NP):
            out.append(jnp.where(half == 0, pairs[q], turned[q]))
            out.append(jnp.where(half == 0, turned[q], pairs[q]))
        return out

    def paired(values):
        return [jnp.where(half == 0, values[2 * p], values[2 * p + 1]) for p in range(NP)]

    def load_dup(kind, t):
        return [
            [dupc[(kind * NV + v) * NV + w, rows_of(t), :] for w in range(NV)] for v in range(NV)
        ]

    def shifted(kind, values, by):
        if kind == 0:
            return [jnp.where(segment < by, 0.0, pltpu.roll(x, by, 0)) for x in values]
        return [jnp.where(segment >= SEG - by, 0.0, pltpu.roll(x, SEG - by, 0)) for x in values]

    unit = [
        [jnp.where(2 * q + half == u, 1.0, 0.0).astype(f32) for q in range(NP)] for u in range(NV)
    ]
    for kind in (0, 1):

        def transfer(i, columns):
            t = i if kind == 0 else steps - 1 - i
            coefs = load_dup(kind, t)
            straight = [
                [
                    jnp.where(half == 0, coefs[2 * p][2 * q], coefs[2 * p + 1][2 * q + 1])
                    for q in range(NP)
                ]
                for p in range(NP)
            ]
            cross = [
                [
                    jnp.where(half == 0, coefs[2 * p][2 * q + 1], coefs[2 * p + 1][2 * q])
                    for q in range(NP)
                ]
                for p in range(NP)
            ]
            new = []
            for u in range(NV):
                turned = crossed(columns[u])
                got = []
                for p in range(NP):
                    terms = [straight[p][q] * columns[u][q] for q in range(NP)]
                    terms += [cross[p][q] * turned[q] for q in range(NP)]
                    got.append(add_up(terms))
                    trans[(kind * NV + u) * NP + p, rows_of(t), :] = got[p]
                new.append(got)
            return new

        last = lax.fori_loop(0, steps, transfer, unit, unroll=2)
        over = [shifted(kind, spread(last[u]), 1) for u in range(NV)]
        for level in range(3):
            for u in range(NV):
                for v in range(NV):
                    jump[((kind * 3 + level) * NV + v) * NV + u] = over[u][v]
            if level < 2:
                before = [shifted(kind, over[u], 1 << level) for u in range(NV)]
                over = [
                    [
                        add_up([over[w][v] * before[u][w] for w in range(NV)])
                        for v in range(NV)
                    ]
                    for u in range(NV)
                ]

    order_forcing = select_columns(forcing[...].reshape(NV * stations, radial), order)
    for copy in halos:
        copy.wait_recv()
    for v in range(NV):
        line[v, 8 + stations : 9 + stations, :] = jnp.where(
            here == spaces - 1, 0.0, halo_in[0, v : v + 1, :]
        )
        line[v, 7:8, :] = jnp.where(here == 0, 0.0, halo_in[1, v : v + 1, :])

    spot = lax.broadcasted_iota(jnp.int32, (8, radial), 1)

    def local(i, carry):
        at = pl.multiple_of(i * 8, 8)
        axial, outward, mean = [], [], []
        for v in range(NV):
            window = line[v, pl.ds(at, 24), :]
            centre = window[8:16]
            ahead = window[9:17]
            behind = window[7:15]
            outer = jnp.where(spot == radial - 1, 0.0, pltpu.roll(centre, radial - 1, 1))
            inner = jnp.where(spot == 0, 0.0, pltpu.roll(centre, 1, 1))
            axial.append(0.5 * (ahead - behind))
            outward.append(0.5 * (outer - inner))
            mean.append(damping * (ahead + behind + outer + inner - 4.0 * centre))
        for v in range(NV):
            total = ajac[v, 0] * axial[0] + rjac[v, 0] * outward[0]
            for w in range(1, NV):
                total = total + (ajac[v, w] * axial[w] + rjac[v, w] * outward[w])
            base[v, pl.ds(at, 8), :] = total - mean[v]
        return carry

    lax.fori_loop(0, stations // 8, local, 0)
    for v in range(NV):
        base[v] = base[v] - order_forcing[v * stations : (v + 1) * stations]

    for copy in second:
        copy.wait_recv()

    pairs = []
    for p in range(NP):
        blocks = []
        for v in (2 * p, 2 * p + 1):
            timed = jnp.concatenate(
                [recv2[e, v * per : (v + 1) * per, :] for e in range(count)], axis=0
            )
            residual = base[v] + timed
            res_out[v] = residual
            blocks.append(residual)
        sweep0[p] = jnp.concatenate(blocks, axis=0).T

    zeros = [jnp.zeros((SEG, 128), f32) for _ in range(NV)]

    def add_transfer(kind, t, start, entering):
        return [
            add_up(
                [start[p]]
                + [
                    trans[(kind * NV + u) * NP + p, rows_of(t), :] * entering[u]
                    for u in range(NV)
                ]
            )
            for p in range(NP)
        ]

    def advance(coefs, held, start):
        return [
            add_up([coefs[v][w] * held[w] for w in range(NV)]) + start[v] for v in range(NV)
        ]

    def carries(kind, ends):
        held = shifted(kind, ends, 1)
        for level in range(3):
            base_at = (kind * 3 + level) * NV * NV
            coefs = [[jump[base_at + v * NV + u] for u in range(NV)] for v in range(NV)]
            held = advance(coefs, shifted(kind, held, 1 << level), held)
        return held

    def forward(t, held):
        source = [sweep0[p, at_step(t), :] for p in range(NP)]
        turned = crossed(source)
        start = []
        for p in range(NP):
            terms = []
            for q in range(NP):
                at = (p * NP + q) * 2
                terms.append(pairc[at, rows_of(t), :] * source[q])
                terms.append(pairc[at + 1, rows_of(t), :] * turned[q])
            start.append(add_up(terms))
        got = advance(load_dup(0, t), held, spread(start))
        for p, x in enumerate(paired(got)):
            sweep1[p, rows_of(t), :] = x
        return got

    ends = lax.fori_loop(0, steps, forward, zeros, unroll=True)
    entering = carries(0, ends)

    def backward(i, held):
        t = steps - 1 - i
        start = add_transfer(0, t, [sweep1[p, rows_of(t), :] for p in range(NP)], entering)
        got = advance(load_dup(1, t), held, spread(start))
        for p, x in enumerate(paired(got)):
            sweep0[p, rows_of(t), :] = x
        return got

    ends = lax.fori_loop(0, steps, backward, zeros, unroll=True)
    leaving = carries(1, ends)

    def finish(t, carry):
        got = add_transfer(1, t, [sweep0[p, rows_of(t), :] for p in range(NP)], leaving)
        for p in range(NP):
            sweep1[p, at_step(t), :] = got[p]
        return carry

    lax.fori_loop(0, steps, finish, 0, unroll=4)
    for p in range(NP):
        block = sweep1[p].T
        cor_out[2 * p] = block[:stations]
        cor_out[2 * p + 1] = block[stations:]

    for copy in first + halos + second:
        copy.wait_send()


def deliver(residual, correction, res_out, cor_out, sem):
    copies = [
        pltpu.make_async_copy(residual, res_out, sem.at[0]),
        pltpu.make_async_copy(correction, cor_out, sem.at[1]),
    ]
    for copy in copies:
        copy.start()
    for copy in copies:
        copy.wait()


def shards(
    count,
    spaces,
    flow_state,
    forcing,
    pivot_table,
    block_offset,
    line_perm,
    axial_jac,
    radial_jac,
    lower_block,
    upper_block,
):
    _, variables, stations, radial = flow_state.shape
    per = stations // count
    block = jax.ShapeDtypeStruct((variables, stations, radial), f32)
    vmem = pl.BlockSpec(memory_space=pltpu.VMEM)
    dma = pltpu.SemaphoreType.DMA
    exchanged = pltpu.VMEM((count, variables * per, radial), f32)
    residual, correction = pl.pallas_call(
        functools.partial(kernel, count, spaces),
        out_shape=(block, block),
        in_specs=[pl.BlockSpec(memory_space=pltpu.HBM)] * 9,
        out_specs=(vmem, vmem),
        scratch_shapes=[
            pltpu.VMEM((variables, stations, radial), f32),
            pltpu.VMEM((variables, stations, radial), f32),
            pltpu.VMEM((variables, variables, 8, radial), f32),
            pltpu.VMEM((1, stations), jnp.int32),
            pltpu.VMEM((1, radial), jnp.int32),
            pltpu.SMEM((variables, variables), f32),
            pltpu.SMEM((variables, variables), f32),
            pltpu.SMEM((variables, variables), f32),
            pltpu.SMEM((variables, variables), f32),
            dma((9,)),
            pltpu.VMEM((variables, stations + 16, radial), f32),
            pltpu.VMEM((variables, stations, radial), f32),
            exchanged,
            exchanged,
            exchanged,
            exchanged,
            pltpu.VMEM((2, variables, radial), f32),
            pltpu.VMEM((2, variables, radial), f32),
            pltpu.VMEM((1024, radial), f32),
            pltpu.VMEM((24, radial, 128), f32),
            pltpu.VMEM((80, radial, 128), f32),
            pltpu.VMEM((36, radial, 128), f32),
            pltpu.VMEM((6 * variables * variables, SEG, 128), f32),
            pltpu.VMEM((12, 256, 256), jnp.bfloat16),
            pltpu.VMEM((1024, 256), jnp.bfloat16),
            pltpu.VMEM((NP, radial, 128), f32),
            pltpu.VMEM((NP, radial, 128), f32),
            dma((count - 1,)),
            dma((count - 1,)),
            dma((count - 1,)),
            dma((count - 1,)),
            dma((2,)),
            dma((2,)),
            pltpu.SemaphoreType.REGULAR,
        ],
        compiler_params=pltpu.CompilerParams(
            collective_id=0, has_side_effects=True, vmem_limit_bytes=32 * 1024 * 1024
        ),
    )(
        *(
            pltpu.with_memory_space_constraint(x, pltpu.HBM)
            for x in (
                flow_state[0],
                forcing[0],
                jnp.transpose(pivot_table, (1, 2, 0, 3)),
                block_offset.reshape(1, stations),
                line_perm.reshape(1, radial),
                axial_jac,
                radial_jac,
                lower_block,
                upper_block,
            )
        )
    )
    anywhere = pl.BlockSpec(memory_space=pl.ANY)
    residual, correction = pl.pallas_call(
        deliver,
        out_shape=(block, block),
        in_specs=[vmem] * 2,
        out_specs=(anywhere, anywhere),
        scratch_shapes=[dma((2,))],
    )(
        pltpu.with_memory_space_constraint(residual, pltpu.VMEM),
        pltpu.with_memory_space_constraint(correction, pltpu.VMEM),
    )
    return residual[None], correction[None]


def solution(mesh):
    spec = P("inst", None, "space", None)
    return jax.shard_map(
        functools.partial(shards, mesh.shape["inst"], mesh.shape["space"]),
        mesh=mesh,
        in_specs=(spec, spec, P(), P("space"), P(), P(), P(), P(), P()),
        out_specs=(spec, spec),
        check_vma=False,
    )
```

```python
import functools

import jax
import jax.numpy as jnp
import numpy as np
from jax import lax
from jax.experimental import pallas as pl
from jax.experimental.pallas import tpu as pltpu
from jax.sharding import PartitionSpec as P

frequency = 0.5
viscosity = 0.01
damping = 0.25

f32 = jnp.float32
MESH = pl.DeviceIdType.MESH
NV = 6
NP = NV // 2
SEG = 8


def spectral_matrix(count):
    index = np.arange(count)
    distance = index[:, None] - index[None, :]
    parity = 1.0 - 2.0 * (distance % 2)
    angle = np.pi * distance / count
    diagonal = distance == 0
    sine = np.where(diagonal, 1.0, np.sin(angle))
    first = np.where(diagonal, 0.0, 0.5 * parity * np.cos(angle) / sine)
    second = np.where(diagonal, -(count * count + 2) / 12.0, -0.5 * parity / (sine * sine))
    return (frequency * first - viscosity * second).astype(np.float32)


def select_columns(x, onehot):
    high = x.astype(jnp.bfloat16)
    rest = x - high.astype(f32)
    middle = rest.astype(jnp.bfloat16)
    low = (rest - middle.astype(f32)).astype(jnp.bfloat16)
    out = jnp.dot(high, onehot, preferred_element_type=f32)
    out = out + jnp.dot(middle, onehot, preferred_element_type=f32)
    return out + jnp.dot(low, onehot, preferred_element_type=f32)


def kernel(
    count,
    spaces,
    state_in,
    forcing_in,
    pivot_in,
    offset_in,
    perm_in,
    ajac_in,
    rjac_in,
    lower_in,
    upper_in,
    res_out,
    cor_out,
    state,
    forcing,
    pivot,
    offset,
    perm,
    ajac,
    rjac,
    lower,
    upper,
    insem,
    line,
    base,
    send1,
    recv1,
    send2,
    recv2,
    halo_out,
    halo_in,
    tab,
    pairc,
    dupc,
    trans,
    jump,
    rhs,
    pieces,
    sweep0,
    sweep1,
    ssem1,
    rsem1,
    ssem2,
    rsem2,
    hssem,
    hrsem,
    go,
):
    sources = (
        perm_in, state_in, pivot_in, offset_in, lower_in, upper_in, ajac_in, rjac_in, forcing_in
    )
    targets = (perm, state, pivot, offset, lower, upper, ajac, rjac, forcing)
    loads = [
        pltpu.make_async_copy(source, target, insem.at[i])
        for i, (source, target) in enumerate(zip(sources, targets))
    ]
    for load in loads:
        load.start()
    stations, radial = state.shape[1], state.shape[2]
    per = stations // count
    steps = radial // SEG
    spectral = spectral_matrix(count)
    me = lax.axis_index("inst")
    here = lax.axis_index("space")
    up = lax.rem(here + 1, spaces)
    down = lax.rem(here + spaces - 1, spaces)

    barrier = pltpu.get_barrier_semaphore()
    gate, informer = count - 1, count - 2
    for n in range(gate):

        @pl.when(me != n)
        def _():
            pl.semaphore_signal(barrier, inc=1, device_id={"inst": n}, device_id_type=MESH)

    for other in (up, down):
        pl.semaphore_signal(
            barrier, inc=1, device_id={"inst": gate, "space": other}, device_id_type=MESH
        )

    loads[0].wait()
    rows = lax.broadcasted_iota(jnp.int32, (radial, radial), 0)
    order = (rows == perm[...]).astype(f32).astype(jnp.bfloat16)
    loads[1].wait()
    flat = select_columns(state[...].reshape(NV * stations, radial), order)
    for v in range(NV):
        block = flat[v * stations : (v + 1) * stations]
        line[v, 8 : 8 + stations, :] = block
        halo_out[0, v : v + 1, :] = block[0:1]
        halo_out[1, v : v + 1, :] = block[stations - 1 : stations]
        for e in range(count):
            at = v % NP * per
            send1[v // NP, e, at : at + per, :] = block[e * per : (e + 1) * per]

    @pl.when(me != gate)
    def _():
        pl.semaphore_wait(barrier, count - 1)

    @pl.when(me == informer)
    def _():
        pl.semaphore_signal(go, inc=1, device_id={"inst": gate}, device_id_type=MESH)

    @pl.when(me == gate)
    def _():
        pl.semaphore_wait(go, 1)

    def exchange(part, source, target, ssem, rsem):
        copies = []
        for d in range(count - 1, 0, -1):
            other = lax.rem(me + d, count)
            copies.append(
                pltpu.make_async_remote_copy(
                    src_ref=source.at[part, other],
                    dst_ref=target.at[part, me],
                    send_sem=ssem.at[part, d - 1],
                    recv_sem=rsem.at[part, d - 1],
                    device_id={"inst": other},
                    device_id_type=MESH,
                )
            )
        return copies

    first = [exchange(part, send1, recv1, ssem1, rsem1) for part in (0, 1)]
    for copy in first[0] + first[1]:
        copy.start()
    halos = []
    for side, other in ((0, down), (1, up)):
        halos.append(
            pltpu.make_async_remote_copy(
                src_ref=halo_out.at[side],
                dst_ref=halo_in.at[side],
                send_sem=hssem.at[side],
                recv_sem=hrsem.at[side],
                device_id={"space": other},
                device_id_type=MESH,
            )
        )
    for part in (0, 1):
        recv1[part, me] = send1[part, me]

    for load in loads[2:]:
        load.wait()
    for v in range(NV):
        for w in range(NV):
            at = (((v // 2 * NP + w // 2) * 2 + (v % 2 ^ w % 2)) * 2 + v % 2) * 8
            tab[at : at + 8, :] = pivot[v, w]
    tab[288:384, :] = jnp.zeros((96, radial), f32)
    tab[960:, :] = jnp.zeros((64, radial), f32)
    for kind, matrix in ((0, lower), (1, upper)):
        for v in range(NV):
            parts = [pivot[v, u] for u in range(NV)]
            for w in range(NV):
                total = parts[0] * matrix[0, w]
                for u in range(1, NV):
                    total = total + parts[u] * matrix[u, w]
                at = 384 + ((kind * NV + v) * NV + w) * 8
                tab[at : at + 8, :] = -total

    lane = lax.broadcasted_iota(jnp.int32, (32, 256), 1)
    row = lax.broadcasted_iota(jnp.int32, (32, 256), 0)
    wanted = jnp.concatenate([offset[...]] * 4, axis=1)
    rhs[...] = jnp.zeros_like(rhs)
    hit = (row == (lane // 64) * 8 + wanted).astype(f32).astype(jnp.bfloat16)
    for g in range(4):
        for piece in (0, 128):
            rhs[g, piece + 32 * g : piece + 32 * g + 32, :] = hit
    hit = (row == (lane // 128) * 8 + wanted)[:16].astype(f32).astype(jnp.bfloat16)
    for g in range(8):
        for piece in (0, 128):
            rhs[4 + g, piece + 16 * g : piece + 16 * g + 16, :] = hit
    target = lax.broadcasted_iota(jnp.int32, (radial, radial), 0)
    origin = lax.broadcasted_iota(jnp.int32, (radial, radial), 1)
    regroup = (origin == (target % SEG) * steps + target // SEG).astype(f32).astype(jnp.bfloat16)

    def split(b, carry):
        at = pl.multiple_of(b * 128, 128)
        block = tab[pl.ds(at, 128), :]
        high = block.astype(jnp.bfloat16)
        low = (block - high.astype(f32)).astype(jnp.bfloat16)
        for i, x in enumerate((high, low)):
            pieces[pl.ds(at, 128), i * 128 : i * 128 + 128] = lax.dot_general(
                regroup, x, (((1,), (1,)), ((), ())), preferred_element_type=f32
            ).astype(jnp.bfloat16)
        return carry

    lax.fori_loop(0, 8, split, 0, unroll=2)

    @pl.when(me == gate)
    def _():
        pl.semaphore_wait(barrier, 2 * count)
        for n in range(gate):
            pl.semaphore_signal(go, inc=1, device_id={"inst": n}, device_id_type=MESH)

    def expand(first_block, blocks, first_rhs, groups, into):
        def body(g, carry):
            both = jnp.dot(
                pieces[first_block * 128 : (first_block + blocks) * 128, :],
                rhs[first_rhs + g],
                preferred_element_type=f32,
            )
            for b in range(blocks):
                into[(b * groups + g) * 2] = both[b * 128 : b * 128 + 128, :128]
                into[(b * groups + g) * 2 + 1] = both[b * 128 : b * 128 + 128, 128:]
            return carry

        lax.fori_loop(0, groups, body, 0)

    expand(0, 3, 0, 4, pairc)
    expand(3, 5, 4, 8, dupc)

    @pl.when(me != gate)
    def _():
        pl.semaphore_wait(go, 1)

    for copy in halos:
        copy.start()

    second = [exchange(part, send2, recv2, ssem2, rsem2) for part in (0, 1)]
    for part in (0, 1):
        for copy in first[part]:
            copy.wait_recv()
        for n in range(count):
            total = float(spectral[n, 0]) * recv1[part, 0]
            for m in range(1, count):
                total = total + float(spectral[n, m]) * recv1[part, m]
            send2[part, n] = total
        for copy in second[part]:
            copy.start()
        recv2[part, me] = send2[part, me]

    def at_step(t):
        return pl.ds(t, SEG, stride=steps)

    def rows_of(t):
        return pl.ds(pl.multiple_of(t * SEG, SEG), SEG)

    def crossed(pairs):
        return [pltpu.roll(x, 64, 1) for x in pairs]

    def add_up(terms):
        while len(terms) > 1:
            terms = [sum(terms[i : i + 2][1:], terms[i]) for i in range(0, len(terms), 2)]
        return terms[0]

    half = lax.broadcasted_iota(jnp.int32, (SEG, 128), 1) // 64
    segment = lax.broadcasted_iota(jnp.int32, (SEG, 128), 0)

    def spread(pairs):
        turned = crossed(pairs)
        out = []
        for q in range(NP):
            out.append(jnp.where(half == 0, pairs[q], turned[q]))
            out.append(jnp.where(half == 0, turned[q], pairs[q]))
        return out

    def paired(values):
        return [jnp.where(half == 0, values[2 * p], values[2 * p + 1]) for p in range(NP)]

    def load_dup(kind, t):
        return [
            [dupc[(kind * NV + v) * NV + w, rows_of(t), :] for w in range(NV)] for v in range(NV)
        ]

    def shifted(kind, values, by):
        if kind == 0:
            return [jnp.where(segment < by, 0.0, pltpu.roll(x, by, 0)) for x in values]
        return [jnp.where(segment >= SEG - by, 0.0, pltpu.roll(x, SEG - by, 0)) for x in values]

    unit = [
        [jnp.where(2 * q + half == u, 1.0, 0.0).astype(f32) for q in range(NP)] for u in range(NV)
    ]
    for kind in (0, 1):

        def transfer(i, columns):
            t = i if kind == 0 else steps - 1 - i
            coefs = load_dup(kind, t)
            straight = [
                [
                    jnp.where(half == 0, coefs[2 * p][2 * q], coefs[2 * p + 1][2 * q + 1])
                    for q in range(NP)
                ]
                for p in range(NP)
            ]
            cross = [
                [
                    jnp.where(half == 0, coefs[2 * p][2 * q + 1], coefs[2 * p + 1][2 * q])
                    for q in range(NP)
                ]
                for p in range(NP)
            ]
            new = []
            for u in range(NV):
                turned = crossed(columns[u])
                got = []
                for p in range(NP):
                    terms = [straight[p][q] * columns[u][q] for q in range(NP)]
                    terms += [cross[p][q] * turned[q] for q in range(NP)]
                    got.append(add_up(terms))
                    trans[(kind * NV + u) * NP + p, rows_of(t), :] = got[p]
                new.append(got)
            return new

        last = lax.fori_loop(0, steps, transfer, unit, unroll=2)
        over = [shifted(kind, spread(last[u]), 1) for u in range(NV)]
        for level in range(3):
            for u in range(NV):
                for v in range(NV):
                    jump[((kind * 3 + level) * NV + v) * NV + u] = over[u][v]
            if level < 2:
                before = [shifted(kind, over[u], 1 << level) for u in range(NV)]
                over = [
                    [
                        add_up([over[w][v] * before[u][w] for w in range(NV)])
                        for v in range(NV)
                    ]
                    for u in range(NV)
                ]

    order_forcing = select_columns(forcing[...].reshape(NV * stations, radial), order)
    for copy in halos:
        copy.wait_recv()
    for v in range(NV):
        line[v, 8 + stations : 9 + stations, :] = jnp.where(
            here == spaces - 1, 0.0, halo_in[0, v : v + 1, :]
        )
        line[v, 7:8, :] = jnp.where(here == 0, 0.0, halo_in[1, v : v + 1, :])

    spot = lax.broadcasted_iota(jnp.int32, (8, radial), 1)

    def local(i, carry):
        at = pl.multiple_of(i * 8, 8)
        axial, outward, mean = [], [], []
        for v in range(NV):
            window = line[v, pl.ds(at, 24), :]
            centre = window[8:16]
            ahead = window[9:17]
            behind = window[7:15]
            outer = jnp.where(spot == radial - 1, 0.0, pltpu.roll(centre, radial - 1, 1))
            inner = jnp.where(spot == 0, 0.0, pltpu.roll(centre, 1, 1))
            axial.append(0.5 * (ahead - behind))
            outward.append(0.5 * (outer - inner))
            mean.append(damping * (ahead + behind + outer + inner - 4.0 * centre))
        for v in range(NV):
            total = ajac[v, 0] * axial[0] + rjac[v, 0] * outward[0]
            for w in range(1, NV):
                total = total + (ajac[v, w] * axial[w] + rjac[v, w] * outward[w])
            base[v, pl.ds(at, 8), :] = total - mean[v]
        return carry

    lax.fori_loop(0, stations // 8, local, 0)
    for v in range(NV):
        base[v] = base[v] - order_forcing[v * stations : (v + 1) * stations]

    for copy in second[0] + second[1]:
        copy.wait_recv()

    pairs = []
    for p in range(NP):
        blocks = []
        for v in (2 * p, 2 * p + 1):
            timed = jnp.concatenate(
                [
                    recv2[v // NP, e, v % NP * per : (v % NP + 1) * per, :]
                    for e in range(count)
                ],
                axis=0,
            )
            residual = base[v] + timed
            res_out[v] = residual
            blocks.append(residual)
        sweep0[p] = jnp.concatenate(blocks, axis=0).T

    zeros = [jnp.zeros((SEG, 128), f32) for _ in range(NV)]

    def add_transfer(kind, t, start, entering):
        return [
            add_up(
                [start[p]]
                + [
                    trans[(kind * NV + u) * NP + p, rows_of(t), :] * entering[u]
                    for u in range(NV)
                ]
            )
            for p in range(NP)
        ]

    def advance(coefs, held, start):
        return [
            add_up([coefs[v][w] * held[w] for w in range(NV)]) + start[v] for v in range(NV)
        ]

    def carries(kind, ends):
        held = shifted(kind, ends, 1)
        for level in range(3):
            base_at = (kind * 3 + level) * NV * NV
            coefs = [[jump[base_at + v * NV + u] for u in range(NV)] for v in range(NV)]
            held = advance(coefs, shifted(kind, held, 1 << level), held)
        return held

    def forward(t, held):
        source = [sweep0[p, at_step(t), :] for p in range(NP)]
        turned = crossed(source)
        start = []
        for p in range(NP):
            terms = []
            for q in range(NP):
                at = (p * NP + q) * 2
                terms.append(pairc[at, rows_of(t), :] * source[q])
                terms.append(pairc[at + 1, rows_of(t), :] * turned[q])
            start.append(add_up(terms))
        got = advance(load_dup(0, t), held, spread(start))
        for p, x in enumerate(paired(got)):
            sweep1[p, rows_of(t), :] = x
        return got

    ends = lax.fori_loop(0, steps, forward, zeros, unroll=True)
    entering = carries(0, ends)

    def backward(i, held):
        t = steps - 1 - i
        start = add_transfer(0, t, [sweep1[p, rows_of(t), :] for p in range(NP)], entering)
        got = advance(load_dup(1, t), held, spread(start))
        for p, x in enumerate(paired(got)):
            sweep0[p, rows_of(t), :] = x
        return got

    ends = lax.fori_loop(0, steps, backward, zeros, unroll=True)
    leaving = carries(1, ends)

    def finish(t, carry):
        got = add_transfer(1, t, [sweep0[p, rows_of(t), :] for p in range(NP)], leaving)
        for p in range(NP):
            sweep1[p, at_step(t), :] = got[p]
        return carry

    lax.fori_loop(0, steps, finish, 0, unroll=4)
    for p in range(NP):
        block = sweep1[p].T
        cor_out[2 * p] = block[:stations]
        cor_out[2 * p + 1] = block[stations:]

    for copy in first[0] + first[1] + halos + second[0] + second[1]:
        copy.wait_send()


def deliver(residual, correction, res_out, cor_out, sem):
    copies = [
        pltpu.make_async_copy(residual, res_out, sem.at[0]),
        pltpu.make_async_copy(correction, cor_out, sem.at[1]),
    ]
    for copy in copies:
        copy.start()
    for copy in copies:
        copy.wait()


def shards(
    count,
    spaces,
    flow_state,
    forcing,
    pivot_table,
    block_offset,
    line_perm,
    axial_jac,
    radial_jac,
    lower_block,
    upper_block,
):
    _, variables, stations, radial = flow_state.shape
    per = stations // count
    block = jax.ShapeDtypeStruct((variables, stations, radial), f32)
    vmem = pl.BlockSpec(memory_space=pltpu.VMEM)
    dma = pltpu.SemaphoreType.DMA
    exchanged = pltpu.VMEM((2, count, NP * per, radial), f32)
    residual, correction = pl.pallas_call(
        functools.partial(kernel, count, spaces),
        out_shape=(block, block),
        in_specs=[pl.BlockSpec(memory_space=pltpu.HBM)] * 9,
        out_specs=(vmem, vmem),
        scratch_shapes=[
            pltpu.VMEM((variables, stations, radial), f32),
            pltpu.VMEM((variables, stations, radial), f32),
            pltpu.VMEM((variables, variables, 8, radial), f32),
            pltpu.VMEM((1, stations), jnp.int32),
            pltpu.VMEM((1, radial), jnp.int32),
            pltpu.SMEM((variables, variables), f32),
            pltpu.SMEM((variables, variables), f32),
            pltpu.SMEM((variables, variables), f32),
            pltpu.SMEM((variables, variables), f32),
            dma((9,)),
            pltpu.VMEM((variables, stations + 16, radial), f32),
            pltpu.VMEM((variables, stations, radial), f32),
            exchanged,
            exchanged,
            exchanged,
            exchanged,
            pltpu.VMEM((2, variables, radial), f32),
            pltpu.VMEM((2, variables, radial), f32),
            pltpu.VMEM((1024, radial), f32),
            pltpu.VMEM((24, radial, 128), f32),
            pltpu.VMEM((80, radial, 128), f32),
            pltpu.VMEM((36, radial, 128), f32),
            pltpu.VMEM((6 * variables * variables, SEG, 128), f32),
            pltpu.VMEM((12, 256, 256), jnp.bfloat16),
            pltpu.VMEM((1024, 256), jnp.bfloat16),
            pltpu.VMEM((NP, radial, 128), f32),
            pltpu.VMEM((NP, radial, 128), f32),
            dma((2, count - 1)),
            dma((2, count - 1)),
            dma((2, count - 1)),
            dma((2, count - 1)),
            dma((2,)),
            dma((2,)),
            pltpu.SemaphoreType.REGULAR,
        ],
        compiler_params=pltpu.CompilerParams(
            collective_id=0, has_side_effects=True, vmem_limit_bytes=32 * 1024 * 1024
        ),
    )(
        *(
            pltpu.with_memory_space_constraint(x, pltpu.HBM)
            for x in (
                flow_state[0],
                forcing[0],
                jnp.transpose(pivot_table, (1, 2, 0, 3)),
                block_offset.reshape(1, stations),
                line_perm.reshape(1, radial),
                axial_jac,
                radial_jac,
                lower_block,
                upper_block,
            )
        )
    )
    anywhere = pl.BlockSpec(memory_space=pl.ANY)
    residual, correction = pl.pallas_call(
        deliver,
        out_shape=(block, block),
        in_specs=[vmem] * 2,
        out_specs=(anywhere, anywhere),
        scratch_shapes=[dma((2,))],
    )(
        pltpu.with_memory_space_constraint(residual, pltpu.VMEM),
        pltpu.with_memory_space_constraint(correction, pltpu.VMEM),
    )
    return residual[None], correction[None]


def solution(mesh):
    spec = P("inst", None, "space", None)
    return jax.shard_map(
        functools.partial(shards, mesh.shape["inst"], mesh.shape["space"]),
        mesh=mesh,
        in_specs=(spec, spec, P(), P("space"), P(), P(), P(), P(), P()),
        out_specs=(spec, spec),
        check_vma=False,
    )
```

```python
import functools

import jax
import jax.numpy as jnp
import numpy as np
from jax import lax
from jax.experimental import pallas as pl
from jax.experimental.pallas import tpu as pltpu
from jax.sharding import PartitionSpec as P

frequency = 0.5
viscosity = 0.01
damping = 0.25

f32 = jnp.float32
MESH = pl.DeviceIdType.MESH
NV = 6
NP = NV // 2
SEG = 8


def spectral_matrix(count):
    index = np.arange(count)
    distance = index[:, None] - index[None, :]
    parity = 1.0 - 2.0 * (distance % 2)
    angle = np.pi * distance / count
    diagonal = distance == 0
    sine = np.where(diagonal, 1.0, np.sin(angle))
    first = np.where(diagonal, 0.0, 0.5 * parity * np.cos(angle) / sine)
    second = np.where(diagonal, -(count * count + 2) / 12.0, -0.5 * parity / (sine * sine))
    return (frequency * first - viscosity * second).astype(np.float32)


def select_columns(x, onehot):
    high = x.astype(jnp.bfloat16)
    rest = x - high.astype(f32)
    middle = rest.astype(jnp.bfloat16)
    low = (rest - middle.astype(f32)).astype(jnp.bfloat16)
    out = jnp.dot(high, onehot, preferred_element_type=f32)
    out = out + jnp.dot(middle, onehot, preferred_element_type=f32)
    return out + jnp.dot(low, onehot, preferred_element_type=f32)


def kernel(
    count,
    spaces,
    state_in,
    forcing_in,
    pivot_in,
    offset_in,
    perm_in,
    ajac_in,
    rjac_in,
    lower_in,
    upper_in,
    res_out,
    cor_out,
    state,
    forcing,
    pivot,
    offset,
    perm,
    ajac,
    rjac,
    lower,
    upper,
    insem,
    line,
    base,
    send1,
    recv1,
    send2,
    recv2,
    halo_out,
    halo_in,
    tab,
    pairc,
    dupc,
    trans,
    jump,
    rhs,
    pieces,
    sweep0,
    sweep1,
    ssem1,
    rsem1,
    ssem2,
    rsem2,
    hssem,
    hrsem,
    go,
):
    sources = (
        perm_in, state_in, pivot_in, offset_in, lower_in, upper_in, ajac_in, rjac_in, forcing_in
    )
    targets = (perm, state, pivot, offset, lower, upper, ajac, rjac, forcing)
    loads = [
        pltpu.make_async_copy(source, target, insem.at[i])
        for i, (source, target) in enumerate(zip(sources, targets))
    ]
    for load in loads:
        load.start()
    stations, radial = state.shape[1], state.shape[2]
    per = stations // count
    steps = radial // SEG
    spectral = spectral_matrix(count)
    me = lax.axis_index("inst")
    here = lax.axis_index("space")
    up = lax.rem(here + 1, spaces)
    down = lax.rem(here + spaces - 1, spaces)

    barrier = pltpu.get_barrier_semaphore()
    gate, informer = count - 1, count - 2
    for n in range(gate):

        @pl.when(me != n)
        def _():
            pl.semaphore_signal(barrier, inc=1, device_id={"inst": n}, device_id_type=MESH)

    for other in (up, down):
        pl.semaphore_signal(
            barrier, inc=1, device_id={"inst": gate, "space": other}, device_id_type=MESH
        )

    loads[0].wait()
    rows = lax.broadcasted_iota(jnp.int32, (radial, radial), 0)
    order = (rows == perm[...]).astype(f32).astype(jnp.bfloat16)
    loads[1].wait()
    flat = select_columns(state[...].reshape(NV * stations, radial), order)
    for v in range(NV):
        block = flat[v * stations : (v + 1) * stations]
        line[v, 8 : 8 + stations, :] = block
        halo_out[0, v : v + 1, :] = block[0:1]
        halo_out[1, v : v + 1, :] = block[stations - 1 : stations]
        for e in range(count):
            at = v % NP * per
            send1[v // NP, e, at : at + per, :] = block[e * per : (e + 1) * per]

    @pl.when(me != gate)
    def _():
        pl.semaphore_wait(barrier, count - 1)

    @pl.when(me == informer)
    def _():
        pl.semaphore_signal(go, inc=1, device_id={"inst": gate}, device_id_type=MESH)

    @pl.when(me == gate)
    def _():
        pl.semaphore_wait(go, 1)

    def exchange(part, source, target, ssem, rsem):
        copies = []
        for d in range(count - 1, 0, -1):
            other = lax.rem(me + d, count)
            copies.append(
                pltpu.make_async_remote_copy(
                    src_ref=source.at[part, other],
                    dst_ref=target.at[part, me],
                    send_sem=ssem.at[part, d - 1],
                    recv_sem=rsem.at[part, d - 1],
                    device_id={"inst": other},
                    device_id_type=MESH,
                )
            )
        return copies

    first = [exchange(part, send1, recv1, ssem1, rsem1) for part in (0, 1)]
    for copy in first[0] + first[1]:
        copy.start()
    halos = []
    for side, other in ((0, down), (1, up)):
        halos.append(
            pltpu.make_async_remote_copy(
                src_ref=halo_out.at[side],
                dst_ref=halo_in.at[side],
                send_sem=hssem.at[side],
                recv_sem=hrsem.at[side],
                device_id={"space": other},
                device_id_type=MESH,
            )
        )
    for part in (0, 1):
        recv1[part, me] = send1[part, me]

    for load in loads[2:]:
        load.wait()
    for v in range(NV):
        for w in range(NV):
            at = (((v // 2 * NP + w // 2) * 2 + (v % 2 ^ w % 2)) * 2 + v % 2) * 8
            tab[at : at + 8, :] = pivot[v, w]
    tab[288:384, :] = jnp.zeros((96, radial), f32)
    tab[960:, :] = jnp.zeros((64, radial), f32)
    for kind, matrix in ((0, lower), (1, upper)):
        for v in range(NV):
            parts = [pivot[v, u] for u in range(NV)]
            for w in range(NV):
                total = parts[0] * matrix[0, w]
                for u in range(1, NV):
                    total = total + parts[u] * matrix[u, w]
                at = 384 + ((kind * NV + v) * NV + w) * 8
                tab[at : at + 8, :] = -total

    lane = lax.broadcasted_iota(jnp.int32, (32, 256), 1)
    row = lax.broadcasted_iota(jnp.int32, (32, 256), 0)
    wanted = jnp.concatenate([offset[...]] * 4, axis=1)
    rhs[...] = jnp.zeros_like(rhs)
    hit = (row == (lane // 64) * 8 + wanted).astype(f32).astype(jnp.bfloat16)
    for g in range(4):
        for piece in (0, 128):
            rhs[g, piece + 32 * g : piece + 32 * g + 32, :] = hit
    hit = (row == (lane // 128) * 8 + wanted)[:16].astype(f32).astype(jnp.bfloat16)
    for g in range(8):
        for piece in (0, 128):
            rhs[4 + g, piece + 16 * g : piece + 16 * g + 16, :] = hit
    target = lax.broadcasted_iota(jnp.int32, (radial, radial), 0)
    origin = lax.broadcasted_iota(jnp.int32, (radial, radial), 1)
    regroup = (origin == (target % SEG) * steps + target // SEG).astype(f32).astype(jnp.bfloat16)

    def split(b, carry):
        at = pl.multiple_of(b * 128, 128)
        block = tab[pl.ds(at, 128), :]
        high = block.astype(jnp.bfloat16)
        low = (block - high.astype(f32)).astype(jnp.bfloat16)
        for i, x in enumerate((high, low)):
            pieces[pl.ds(at, 128), i * 128 : i * 128 + 128] = lax.dot_general(
                regroup, x, (((1,), (1,)), ((), ())), preferred_element_type=f32
            ).astype(jnp.bfloat16)
        return carry

    lax.fori_loop(0, 8, split, 0, unroll=2)

    def expand(first_block, blocks, first_rhs, groups, into):
        def body(g, carry):
            both = jnp.dot(
                pieces[first_block * 128 : (first_block + blocks) * 128, :],
                rhs[first_rhs + g],
                preferred_element_type=f32,
            )
            for b in range(blocks):
                into[(b * groups + g) * 2] = both[b * 128 : b * 128 + 128, :128]
                into[(b * groups + g) * 2 + 1] = both[b * 128 : b * 128 + 128, 128:]
            return carry

        lax.fori_loop(0, groups, body, 0)

    expand(0, 3, 0, 4, pairc)
    expand(3, 5, 4, 8, dupc)

    second = [exchange(part, send2, recv2, ssem2, rsem2) for part in (0, 1)]
    for part in (0, 1):
        for copy in first[part]:
            copy.wait_recv()
        for n in range(count):
            total = float(spectral[n, 0]) * recv1[part, 0]
            for m in range(1, count):
                total = total + float(spectral[n, m]) * recv1[part, m]
            send2[part, n] = total
        for copy in second[part]:
            copy.start()
        recv2[part, me] = send2[part, me]
        if part == 0:

            @pl.when(me == gate)
            def _():
                pl.semaphore_wait(barrier, 2 * count)
                for n in range(gate):
                    pl.semaphore_signal(go, inc=1, device_id={"inst": n}, device_id_type=MESH)

            @pl.when(me != gate)
            def _():
                pl.semaphore_wait(go, 1)

            for copy in halos:
                copy.start()

    def at_step(t):
        return pl.ds(t, SEG, stride=steps)

    def rows_of(t):
        return pl.ds(pl.multiple_of(t * SEG, SEG), SEG)

    def crossed(pairs):
        return [pltpu.roll(x, 64, 1) for x in pairs]

    def add_up(terms):
        while len(terms) > 1:
            terms = [sum(terms[i : i + 2][1:], terms[i]) for i in range(0, len(terms), 2)]
        return terms[0]

    half = lax.broadcasted_iota(jnp.int32, (SEG, 128), 1) // 64
    segment = lax.broadcasted_iota(jnp.int32, (SEG, 128), 0)

    def spread(pairs):
        turned = crossed(pairs)
        out = []
        for q in range(NP):
            out.append(jnp.where(half == 0, pairs[q], turned[q]))
            out.append(jnp.where(half == 0, turned[q], pairs[q]))
        return out

    def paired(values):
        return [jnp.where(half == 0, values[2 * p], values[2 * p + 1]) for p in range(NP)]

    def load_dup(kind, t):
        return [
            [dupc[(kind * NV + v) * NV + w, rows_of(t), :] for w in range(NV)] for v in range(NV)
        ]

    def shifted(kind, values, by):
        if kind == 0:
            return [jnp.where(segment < by, 0.0, pltpu.roll(x, by, 0)) for x in values]
        return [jnp.where(segment >= SEG - by, 0.0, pltpu.roll(x, SEG - by, 0)) for x in values]

    unit = [
        [jnp.where(2 * q + half == u, 1.0, 0.0).astype(f32) for q in range(NP)] for u in range(NV)
    ]

    def transfer_step(kind, i, columns):
        t = i if kind == 0 else steps - 1 - i
        coefs = load_dup(kind, t)
        straight = [
            [
                jnp.where(half == 0, coefs[2 * p][2 * q], coefs[2 * p + 1][2 * q + 1])
                for q in range(NP)
            ]
            for p in range(NP)
        ]
        cross = [
            [
                jnp.where(half == 0, coefs[2 * p][2 * q + 1], coefs[2 * p + 1][2 * q])
                for q in range(NP)
            ]
            for p in range(NP)
        ]
        new = []
        for u in range(NV):
            turned = crossed(columns[u])
            got = []
            for p in range(NP):
                terms = [straight[p][q] * columns[u][q] for q in range(NP)]
                terms += [cross[p][q] * turned[q] for q in range(NP)]
                got.append(add_up(terms))
                trans[(kind * NV + u) * NP + p, rows_of(t), :] = got[p]
            new.append(got)
        return new

    def transfer(i, both):
        return [transfer_step(kind, i, both[kind]) for kind in (0, 1)]

    lasts = lax.fori_loop(0, steps, transfer, [unit, unit])
    for kind in (0, 1):
        last = lasts[kind]
        over = [shifted(kind, spread(last[u]), 1) for u in range(NV)]
        for level in range(3):
            for u in range(NV):
                for v in range(NV):
                    jump[((kind * 3 + level) * NV + v) * NV + u] = over[u][v]
            if level < 2:
                before = [shifted(kind, over[u], 1 << level) for u in range(NV)]
                over = [
                    [
                        add_up([over[w][v] * before[u][w] for w in range(NV)])
                        for v in range(NV)
                    ]
                    for u in range(NV)
                ]

    order_forcing = select_columns(forcing[...].reshape(NV * stations, radial), order)
    for copy in halos:
        copy.wait_recv()
    for v in range(NV):
        line[v, 8 + stations : 9 + stations, :] = jnp.where(
            here == spaces - 1, 0.0, halo_in[0, v : v + 1, :]
        )
        line[v, 7:8, :] = jnp.where(here == 0, 0.0, halo_in[1, v : v + 1, :])

    spot = lax.broadcasted_iota(jnp.int32, (8, radial), 1)

    def local(i, carry):
        at = pl.multiple_of(i * 8, 8)
        axial, outward, mean = [], [], []
        for v in range(NV):
            window = line[v, pl.ds(at, 24), :]
            centre = window[8:16]
            ahead = window[9:17]
            behind = window[7:15]
            outer = jnp.where(spot == radial - 1, 0.0, pltpu.roll(centre, radial - 1, 1))
            inner = jnp.where(spot == 0, 0.0, pltpu.roll(centre, 1, 1))
            axial.append(0.5 * (ahead - behind))
            outward.append(0.5 * (outer - inner))
            mean.append(damping * (ahead + behind + outer + inner - 4.0 * centre))
        for v in range(NV):
            total = ajac[v, 0] * axial[0] + rjac[v, 0] * outward[0]
            for w in range(1, NV):
                total = total + (ajac[v, w] * axial[w] + rjac[v, w] * outward[w])
            base[v, pl.ds(at, 8), :] = total - mean[v]
        return carry

    lax.fori_loop(0, stations // 8, local, 0)
    for v in range(NV):
        base[v] = base[v] - order_forcing[v * stations : (v + 1) * stations]

    for copy in second[0] + second[1]:
        copy.wait_recv()

    pairs = []
    for p in range(NP):
        blocks = []
        for v in (2 * p, 2 * p + 1):
            timed = jnp.concatenate(
                [
                    recv2[v // NP, e, v % NP * per : (v % NP + 1) * per, :]
                    for e in range(count)
                ],
                axis=0,
            )
            residual = base[v] + timed
            res_out[v] = residual
            blocks.append(residual)
        sweep0[p] = jnp.concatenate(blocks, axis=0).T

    zeros = [jnp.zeros((SEG, 128), f32) for _ in range(NV)]

    def add_transfer(kind, t, start, entering):
        return [
            add_up(
                [start[p]]
                + [
                    trans[(kind * NV + u) * NP + p, rows_of(t), :] * entering[u]
                    for u in range(NV)
                ]
            )
            for p in range(NP)
        ]

    def advance(coefs, held, start):
        return [
            add_up([coefs[v][w] * held[w] for w in range(NV)]) + start[v] for v in range(NV)
        ]

    def carries(kind, ends):
        held = shifted(kind, ends, 1)
        for level in range(3):
            base_at = (kind * 3 + level) * NV * NV
            coefs = [[jump[base_at + v * NV + u] for u in range(NV)] for v in range(NV)]
            held = advance(coefs, shifted(kind, held, 1 << level), held)
        return held

    def forward(t, held):
        source = [sweep0[p, at_step(t), :] for p in range(NP)]
        turned = crossed(source)
        start = []
        for p in range(NP):
            terms = []
            for q in range(NP):
                at = (p * NP + q) * 2
                terms.append(pairc[at, rows_of(t), :] * source[q])
                terms.append(pairc[at + 1, rows_of(t), :] * turned[q])
            start.append(add_up(terms))
        got = advance(load_dup(0, t), held, spread(start))
        for p, x in enumerate(paired(got)):
            sweep1[p, rows_of(t), :] = x
        return got

    ends = lax.fori_loop(0, steps, forward, zeros, unroll=True)
    entering = carries(0, ends)

    def backward(i, held):
        t = steps - 1 - i
        start = add_transfer(0, t, [sweep1[p, rows_of(t), :] for p in range(NP)], entering)
        got = advance(load_dup(1, t), held, spread(start))
        for p, x in enumerate(paired(got)):
            sweep0[p, rows_of(t), :] = x
        return got

    ends = lax.fori_loop(0, steps, backward, zeros, unroll=True)
    leaving = carries(1, ends)

    def finish(t, carry):
        got = add_transfer(1, t, [sweep0[p, rows_of(t), :] for p in range(NP)], leaving)
        for p in range(NP):
            sweep1[p, at_step(t), :] = got[p]
        return carry

    lax.fori_loop(0, steps, finish, 0, unroll=4)
    for p in range(NP):
        block = sweep1[p].T
        cor_out[2 * p] = block[:stations]
        cor_out[2 * p + 1] = block[stations:]

    for copy in first[0] + first[1] + halos + second[0] + second[1]:
        copy.wait_send()


def deliver(residual, correction, res_out, cor_out, sem):
    copies = [
        pltpu.make_async_copy(residual, res_out, sem.at[0]),
        pltpu.make_async_copy(correction, cor_out, sem.at[1]),
    ]
    for copy in copies:
        copy.start()
    for copy in copies:
        copy.wait()


def shards(
    count,
    spaces,
    flow_state,
    forcing,
    pivot_table,
    block_offset,
    line_perm,
    axial_jac,
    radial_jac,
    lower_block,
    upper_block,
):
    _, variables, stations, radial = flow_state.shape
    per = stations // count
    block = jax.ShapeDtypeStruct((variables, stations, radial), f32)
    vmem = pl.BlockSpec(memory_space=pltpu.VMEM)
    dma = pltpu.SemaphoreType.DMA
    exchanged = pltpu.VMEM((2, count, NP * per, radial), f32)
    residual, correction = pl.pallas_call(
        functools.partial(kernel, count, spaces),
        out_shape=(block, block),
        in_specs=[pl.BlockSpec(memory_space=pltpu.HBM)] * 9,
        out_specs=(vmem, vmem),
        scratch_shapes=[
            pltpu.VMEM((variables, stations, radial), f32),
            pltpu.VMEM((variables, stations, radial), f32),
            pltpu.VMEM((variables, variables, 8, radial), f32),
            pltpu.VMEM((1, stations), jnp.int32),
            pltpu.VMEM((1, radial), jnp.int32),
            pltpu.SMEM((variables, variables), f32),
            pltpu.SMEM((variables, variables), f32),
            pltpu.SMEM((variables, variables), f32),
            pltpu.SMEM((variables, variables), f32),
            dma((9,)),
            pltpu.VMEM((variables, stations + 16, radial), f32),
            pltpu.VMEM((variables, stations, radial), f32),
            exchanged,
            exchanged,
            exchanged,
            exchanged,
            pltpu.VMEM((2, variables, radial), f32),
            pltpu.VMEM((2, variables, radial), f32),
            pltpu.VMEM((1024, radial), f32),
            pltpu.VMEM((24, radial, 128), f32),
            pltpu.VMEM((80, radial, 128), f32),
            pltpu.VMEM((36, radial, 128), f32),
            pltpu.VMEM((6 * variables * variables, SEG, 128), f32),
            pltpu.VMEM((12, 256, 256), jnp.bfloat16),
            pltpu.VMEM((1024, 256), jnp.bfloat16),
            pltpu.VMEM((NP, radial, 128), f32),
            pltpu.VMEM((NP, radial, 128), f32),
            dma((2, count - 1)),
            dma((2, count - 1)),
            dma((2, count - 1)),
            dma((2, count - 1)),
            dma((2,)),
            dma((2,)),
            pltpu.SemaphoreType.REGULAR,
        ],
        compiler_params=pltpu.CompilerParams(
            collective_id=0, has_side_effects=True, vmem_limit_bytes=32 * 1024 * 1024
        ),
    )(
        *(
            pltpu.with_memory_space_constraint(x, pltpu.HBM)
            for x in (
                flow_state[0],
                forcing[0],
                jnp.transpose(pivot_table, (1, 2, 0, 3)),
                block_offset.reshape(1, stations),
                line_perm.reshape(1, radial),
                axial_jac,
                radial_jac,
                lower_block,
                upper_block,
            )
        )
    )
    anywhere = pl.BlockSpec(memory_space=pl.ANY)
    residual, correction = pl.pallas_call(
        deliver,
        out_shape=(block, block),
        in_specs=[vmem] * 2,
        out_specs=(anywhere, anywhere),
        scratch_shapes=[dma((2,))],
    )(
        pltpu.with_memory_space_constraint(residual, pltpu.VMEM),
        pltpu.with_memory_space_constraint(correction, pltpu.VMEM),
    )
    return residual[None], correction[None]


def solution(mesh):
    spec = P("inst", None, "space", None)
    return jax.shard_map(
        functools.partial(shards, mesh.shape["inst"], mesh.shape["space"]),
        mesh=mesh,
        in_specs=(spec, spec, P(), P("space"), P(), P(), P(), P(), P()),
        out_specs=(spec, spec),
        check_vma=False,
    )
```

```python
import functools

import jax
import jax.numpy as jnp
import numpy as np
from jax import lax
from jax.experimental import pallas as pl
from jax.experimental.pallas import tpu as pltpu
from jax.sharding import PartitionSpec as P

frequency = 0.5
viscosity = 0.01
damping = 0.25

f32 = jnp.float32
MESH = pl.DeviceIdType.MESH
NV = 6
NP = NV // 2
SEG = 8


def spectral_matrix(count):
    index = np.arange(count)
    distance = index[:, None] - index[None, :]
    parity = 1.0 - 2.0 * (distance % 2)
    angle = np.pi * distance / count
    diagonal = distance == 0
    sine = np.where(diagonal, 1.0, np.sin(angle))
    first = np.where(diagonal, 0.0, 0.5 * parity * np.cos(angle) / sine)
    second = np.where(diagonal, -(count * count + 2) / 12.0, -0.5 * parity / (sine * sine))
    return (frequency * first - viscosity * second).astype(np.float32)


def select_columns(x, onehot):
    high = x.astype(jnp.bfloat16)
    rest = x - high.astype(f32)
    middle = rest.astype(jnp.bfloat16)
    low = (rest - middle.astype(f32)).astype(jnp.bfloat16)
    out = jnp.dot(high, onehot, preferred_element_type=f32)
    out = out + jnp.dot(middle, onehot, preferred_element_type=f32)
    return out + jnp.dot(low, onehot, preferred_element_type=f32)


def kernel(
    count,
    spaces,
    state_in,
    forcing_in,
    pivot_in,
    offset_in,
    perm_in,
    ajac_in,
    rjac_in,
    lower_in,
    upper_in,
    res_out,
    cor_out,
    state,
    forcing,
    pivot,
    offset,
    perm,
    ajac,
    rjac,
    lower,
    upper,
    insem,
    line,
    base,
    send1,
    recv1,
    send2,
    recv2,
    halo_out,
    halo_in,
    tab,
    pairc,
    dupc,
    trans,
    jump,
    rhs,
    pieces,
    sweep0,
    sweep1,
    ssem1,
    rsem1,
    ssem2,
    rsem2,
    hssem,
    hrsem,
    go,
):
    sources = (
        perm_in, state_in, pivot_in, offset_in, lower_in, upper_in, ajac_in, rjac_in, forcing_in
    )
    targets = (perm, state, pivot, offset, lower, upper, ajac, rjac, forcing)
    loads = [
        pltpu.make_async_copy(source, target, insem.at[i])
        for i, (source, target) in enumerate(zip(sources, targets))
    ]
    for load in loads:
        load.start()
    stations, radial = state.shape[1], state.shape[2]
    per = stations // count
    steps = radial // SEG
    spectral = spectral_matrix(count)
    me = lax.axis_index("inst")
    here = lax.axis_index("space")
    up = lax.rem(here + 1, spaces)
    down = lax.rem(here + spaces - 1, spaces)

    barrier = pltpu.get_barrier_semaphore()
    gate, informer = count - 1, count - 2
    for n in range(gate):

        @pl.when(me != n)
        def _():
            pl.semaphore_signal(barrier, inc=1, device_id={"inst": n}, device_id_type=MESH)

    for other in (up, down):
        pl.semaphore_signal(
            barrier, inc=1, device_id={"inst": gate, "space": other}, device_id_type=MESH
        )

    loads[0].wait()
    rows = lax.broadcasted_iota(jnp.int32, (radial, radial), 0)
    order = (rows == perm[...]).astype(f32).astype(jnp.bfloat16)
    loads[1].wait()
    flat = select_columns(state[...].reshape(NV * stations, radial), order)
    for v in range(NV):
        block = flat[v * stations : (v + 1) * stations]
        line[v, 8 : 8 + stations, :] = block
        halo_out[0, v : v + 1, :] = block[0:1]
        halo_out[1, v : v + 1, :] = block[stations - 1 : stations]
        for e in range(count):
            send1[e, v * per : (v + 1) * per, :] = block[e * per : (e + 1) * per]

    @pl.when(me != gate)
    def _():
        pl.semaphore_wait(barrier, count - 1)

    @pl.when(me == informer)
    def _():
        pl.semaphore_signal(go, inc=1, device_id={"inst": gate}, device_id_type=MESH)

    @pl.when(me == gate)
    def _():
        pl.semaphore_wait(go, 1)

    def exchange(source, target, ssem, rsem):
        copies = []
        for d in range(count - 1, 0, -1):
            other = lax.rem(me + d, count)
            copies.append(
                pltpu.make_async_remote_copy(
                    src_ref=source.at[other],
                    dst_ref=target.at[me],
                    send_sem=ssem.at[d - 1],
                    recv_sem=rsem.at[d - 1],
                    device_id={"inst": other},
                    device_id_type=MESH,
                )
            )
        return copies

    first = exchange(send1, recv1, ssem1, rsem1)
    for copy in first:
        copy.start()
    halos = []
    for side, other in ((0, down), (1, up)):
        halos.append(
            pltpu.make_async_remote_copy(
                src_ref=halo_out.at[side],
                dst_ref=halo_in.at[side],
                send_sem=hssem.at[side],
                recv_sem=hrsem.at[side],
                device_id={"space": other},
                device_id_type=MESH,
            )
        )
    recv1[me] = send1[me]

    for load in loads[2:]:
        load.wait()
    for v in range(NV):
        for w in range(NV):
            at = (((v // 2 * NP + w // 2) * 2 + (v % 2 ^ w % 2)) * 2 + v % 2) * 8
            tab[at : at + 8, :] = pivot[v, w]
    tab[288:384, :] = jnp.zeros((96, radial), f32)
    tab[960:, :] = jnp.zeros((64, radial), f32)
    for kind, matrix in ((0, lower), (1, upper)):
        for v in range(NV):
            parts = [pivot[v, u] for u in range(NV)]
            for w in range(NV):
                total = parts[0] * matrix[0, w]
                for u in range(1, NV):
                    total = total + parts[u] * matrix[u, w]
                at = 384 + ((kind * NV + v) * NV + w) * 8
                tab[at : at + 8, :] = -total

    lane = lax.broadcasted_iota(jnp.int32, (32, 256), 1)
    row = lax.broadcasted_iota(jnp.int32, (32, 256), 0)
    wanted = jnp.concatenate([offset[...]] * 4, axis=1)
    rhs[...] = jnp.zeros_like(rhs)
    hit = (row == (lane // 64) * 8 + wanted).astype(f32).astype(jnp.bfloat16)
    for g in range(4):
        for piece in (0, 128):
            rhs[g, piece + 32 * g : piece + 32 * g + 32, :] = hit
    hit = (row == (lane // 128) * 8 + wanted)[:16].astype(f32).astype(jnp.bfloat16)
    for g in range(8):
        for piece in (0, 128):
            rhs[4 + g, piece + 16 * g : piece + 16 * g + 16, :] = hit
    target = lax.broadcasted_iota(jnp.int32, (radial, radial), 0)
    origin = lax.broadcasted_iota(jnp.int32, (radial, radial), 1)
    regroup = (origin == (target % SEG) * steps + target // SEG).astype(f32).astype(jnp.bfloat16)

    def split(b, carry):
        at = pl.multiple_of(b * 128, 128)
        block = tab[pl.ds(at, 128), :]
        high = block.astype(jnp.bfloat16)
        low = (block - high.astype(f32)).astype(jnp.bfloat16)
        for i, x in enumerate((high, low)):
            pieces[pl.ds(at, 128), i * 128 : i * 128 + 128] = lax.dot_general(
                regroup, x, (((1,), (1,)), ((), ())), preferred_element_type=f32
            ).astype(jnp.bfloat16)
        return carry

    lax.fori_loop(0, 8, split, 0, unroll=2)

    def expand(first_block, blocks, first_rhs, groups, into):
        def body(g, carry):
            both = jnp.dot(
                pieces[first_block * 128 : (first_block + blocks) * 128, :],
                rhs[first_rhs + g],
                preferred_element_type=f32,
            )
            for b in range(blocks):
                into[(b * groups + g) * 2] = both[b * 128 : b * 128 + 128, :128]
                into[(b * groups + g) * 2 + 1] = both[b * 128 : b * 128 + 128, 128:]
            return carry

        lax.fori_loop(0, groups, body, 0)

    expand(0, 3, 0, 4, pairc)
    expand(3, 5, 4, 8, dupc)

    @pl.when(me == gate)
    def _():
        pl.semaphore_wait(barrier, 2 * count)
        for n in range(gate):
            pl.semaphore_signal(go, inc=1, device_id={"inst": n}, device_id_type=MESH)

    @pl.when(me != gate)
    def _():
        pl.semaphore_wait(go, 1)

    for copy in halos:
        copy.start()

    for copy in first:
        copy.wait_recv()
    for n in range(count):
        total = float(spectral[n, 0]) * recv1[0]
        for m in range(1, count):
            total = total + float(spectral[n, m]) * recv1[m]
        send2[n] = total
    second = exchange(send2, recv2, ssem2, rsem2)
    for copy in second:
        copy.start()
    recv2[me] = send2[me]

    def at_step(t):
        return pl.ds(t, SEG, stride=steps)

    def rows_of(t):
        return pl.ds(pl.multiple_of(t * SEG, SEG), SEG)

    def crossed(pairs):
        return [pltpu.roll(x, 64, 1) for x in pairs]

    def add_up(terms):
        while len(terms) > 1:
            terms = [sum(terms[i : i + 2][1:], terms[i]) for i in range(0, len(terms), 2)]
        return terms[0]

    half = lax.broadcasted_iota(jnp.int32, (SEG, 128), 1) // 64
    segment = lax.broadcasted_iota(jnp.int32, (SEG, 128), 0)

    def spread(pairs):
        turned = crossed(pairs)
        out = []
        for q in range(NP):
            out.append(jnp.where(half == 0, pairs[q], turned[q]))
            out.append(jnp.where(half == 0, turned[q], pairs[q]))
        return out

    def paired(values):
        return [jnp.where(half == 0, values[2 * p], values[2 * p + 1]) for p in range(NP)]

    def load_dup(kind, t):
        return [
            [dupc[(kind * NV + v) * NV + w, rows_of(t), :] for w in range(NV)] for v in range(NV)
        ]

    def shifted(kind, values, by):
        if kind == 0:
            return [jnp.where(segment < by, 0.0, pltpu.roll(x, by, 0)) for x in values]
        return [jnp.where(segment >= SEG - by, 0.0, pltpu.roll(x, SEG - by, 0)) for x in values]

    unit = [
        [jnp.where(2 * q + half == u, 1.0, 0.0).astype(f32) for q in range(NP)] for u in range(NV)
    ]
    for kind in (0, 1):

        def transfer(i, columns):
            t = i if kind == 0 else steps - 1 - i
            coefs = load_dup(kind, t)
            straight = [
                [
                    jnp.where(half == 0, coefs[2 * p][2 * q], coefs[2 * p + 1][2 * q + 1])
                    for q in range(NP)
                ]
                for p in range(NP)
            ]
            cross = [
                [
                    jnp.where(half == 0, coefs[2 * p][2 * q + 1], coefs[2 * p + 1][2 * q])
                    for q in range(NP)
                ]
                for p in range(NP)
            ]
            new = []
            for u in range(NV):
                turned = crossed(columns[u])
                got = []
                for p in range(NP):
                    terms = [straight[p][q] * columns[u][q] for q in range(NP)]
                    terms += [cross[p][q] * turned[q] for q in range(NP)]
                    got.append(add_up(terms))
                    trans[(kind * NV + u) * NP + p, rows_of(t), :] = got[p]
                new.append(got)
            return new

        last = lax.fori_loop(0, steps, transfer, unit, unroll=2)
        over = [shifted(kind, spread(last[u]), 1) for u in range(NV)]
        for level in range(3):
            for u in range(NV):
                for v in range(NV):
                    jump[((kind * 3 + level) * NV + v) * NV + u] = over[u][v]
            if level < 2:
                before = [shifted(kind, over[u], 1 << level) for u in range(NV)]
                over = [
                    [
                        add_up([over[w][v] * before[u][w] for w in range(NV)])
                        for v in range(NV)
                    ]
                    for u in range(NV)
                ]

    order_forcing = select_columns(forcing[...].reshape(NV * stations, radial), order)
    for copy in halos:
        copy.wait_recv()
    for v in range(NV):
        line[v, 8 + stations : 9 + stations, :] = jnp.where(
            here == spaces - 1, 0.0, halo_in[0, v : v + 1, :]
        )
        line[v, 7:8, :] = jnp.where(here == 0, 0.0, halo_in[1, v : v + 1, :])

    spot = lax.broadcasted_iota(jnp.int32, (8, radial), 1)

    def local(i, carry):
        at = pl.multiple_of(i * 8, 8)
        axial, outward, mean = [], [], []
        for v in range(NV):
            window = line[v, pl.ds(at, 24), :]
            centre = window[8:16]
            ahead = window[9:17]
            behind = window[7:15]
            outer = jnp.where(spot == radial - 1, 0.0, pltpu.roll(centre, radial - 1, 1))
            inner = jnp.where(spot == 0, 0.0, pltpu.roll(centre, 1, 1))
            axial.append(0.5 * (ahead - behind))
            outward.append(0.5 * (outer - inner))
            mean.append(damping * (ahead + behind + outer + inner - 4.0 * centre))
        for v in range(NV):
            total = ajac[v, 0] * axial[0] + rjac[v, 0] * outward[0]
            for w in range(1, NV):
                total = total + (ajac[v, w] * axial[w] + rjac[v, w] * outward[w])
            base[v, pl.ds(at, 8), :] = total - mean[v]
        return carry

    lax.fori_loop(0, stations // 8, local, 0)
    for v in range(NV):
        base[v] = base[v] - order_forcing[v * stations : (v + 1) * stations]

    for copy in second:
        copy.wait_recv()

    pairs = []
    for p in range(NP):
        blocks = []
        for v in (2 * p, 2 * p + 1):
            timed = jnp.concatenate(
                [recv2[e, v * per : (v + 1) * per, :] for e in range(count)], axis=0
            )
            residual = base[v] + timed
            res_out[v] = residual
            blocks.append(residual)
        sweep0[p] = jnp.concatenate(blocks, axis=0).T

    zeros = [jnp.zeros((SEG, 128), f32) for _ in range(NV)]

    def add_transfer(kind, t, start, entering):
        return [
            add_up(
                [start[p]]
                + [
                    trans[(kind * NV + u) * NP + p, rows_of(t), :] * entering[u]
                    for u in range(NV)
                ]
            )
            for p in range(NP)
        ]

    def advance(coefs, held, start):
        return [
            add_up([coefs[v][w] * held[w] for w in range(NV)]) + start[v] for v in range(NV)
        ]

    def carries(kind, ends):
        held = shifted(kind, ends, 1)
        for level in range(3):
            base_at = (kind * 3 + level) * NV * NV
            coefs = [[jump[base_at + v * NV + u] for u in range(NV)] for v in range(NV)]
            held = advance(coefs, shifted(kind, held, 1 << level), held)
        return held

    def forward(t, held):
        source = [sweep0[p, at_step(t), :] for p in range(NP)]
        turned = crossed(source)
        start = []
        for p in range(NP):
            terms = []
            for q in range(NP):
                at = (p * NP + q) * 2
                terms.append(pairc[at, rows_of(t), :] * source[q])
                terms.append(pairc[at + 1, rows_of(t), :] * turned[q])
            start.append(add_up(terms))
        got = advance(load_dup(0, t), held, spread(start))
        for p, x in enumerate(paired(got)):
            sweep1[p, rows_of(t), :] = x
        return got

    ends = lax.fori_loop(0, steps, forward, zeros, unroll=True)
    entering = carries(0, ends)

    def backward(i, held):
        t = steps - 1 - i
        start = add_transfer(0, t, [sweep1[p, rows_of(t), :] for p in range(NP)], entering)
        got = advance(load_dup(1, t), held, spread(start))
        for p, x in enumerate(paired(got)):
            sweep0[p, rows_of(t), :] = x
        return got

    ends = lax.fori_loop(0, steps, backward, zeros, unroll=True)
    leaving = carries(1, ends)

    def finish(t, carry):
        got = add_transfer(1, t, [sweep0[p, rows_of(t), :] for p in range(NP)], leaving)
        for p in range(NP):
            sweep1[p, at_step(t), :] = got[p]
        return carry

    lax.fori_loop(0, steps, finish, 0, unroll=4)
    for p in range(NP):
        block = sweep1[p].T
        cor_out[2 * p] = block[:stations]
        cor_out[2 * p + 1] = block[stations:]

    for copy in first + halos + second:
        copy.wait_send()


def deliver(residual, correction, res_out, cor_out, sem):
    copies = [
        pltpu.make_async_copy(residual, res_out, sem.at[0]),
        pltpu.make_async_copy(correction, cor_out, sem.at[1]),
    ]
    for copy in copies:
        copy.start()
    for copy in copies:
        copy.wait()


def shards(
    count,
    spaces,
    flow_state,
    forcing,
    pivot_table,
    block_offset,
    line_perm,
    axial_jac,
    radial_jac,
    lower_block,
    upper_block,
):
    _, variables, stations, radial = flow_state.shape
    per = stations // count
    block = jax.ShapeDtypeStruct((variables, stations, radial), f32)
    vmem = pl.BlockSpec(memory_space=pltpu.VMEM)
    dma = pltpu.SemaphoreType.DMA
    exchanged = pltpu.VMEM((count, variables * per, radial), f32)
    residual, correction = pl.pallas_call(
        functools.partial(kernel, count, spaces),
        out_shape=(block, block),
        in_specs=[pl.BlockSpec(memory_space=pltpu.HBM)] * 9,
        out_specs=(vmem, vmem),
        scratch_shapes=[
            pltpu.VMEM((variables, stations, radial), f32),
            pltpu.VMEM((variables, stations, radial), f32),
            pltpu.VMEM((variables, variables, 8, radial), f32),
            pltpu.VMEM((1, stations), jnp.int32),
            pltpu.VMEM((1, radial), jnp.int32),
            pltpu.SMEM((variables, variables), f32),
            pltpu.SMEM((variables, variables), f32),
            pltpu.SMEM((variables, variables), f32),
            pltpu.SMEM((variables, variables), f32),
            dma((9,)),
            pltpu.VMEM((variables, stations + 16, radial), f32),
            pltpu.VMEM((variables, stations, radial), f32),
            exchanged,
            exchanged,
            exchanged,
            exchanged,
            pltpu.VMEM((2, variables, radial), f32),
            pltpu.VMEM((2, variables, radial), f32),
            pltpu.VMEM((1024, radial), f32),
            pltpu.VMEM((24, radial, 128), f32),
            pltpu.VMEM((80, radial, 128), f32),
            pltpu.VMEM((36, radial, 128), f32),
            pltpu.VMEM((6 * variables * variables, SEG, 128), f32),
            pltpu.VMEM((12, 256, 256), jnp.bfloat16),
            pltpu.VMEM((1024, 256), jnp.bfloat16),
            pltpu.VMEM((NP, radial, 128), f32),
            pltpu.VMEM((NP, radial, 128), f32),
            dma((count - 1,)),
            dma((count - 1,)),
            dma((count - 1,)),
            dma((count - 1,)),
            dma((2,)),
            dma((2,)),
            pltpu.SemaphoreType.REGULAR,
        ],
        compiler_params=pltpu.CompilerParams(
            collective_id=0, has_side_effects=True, vmem_limit_bytes=32 * 1024 * 1024
        ),
    )(
        *(
            pltpu.with_memory_space_constraint(x, pltpu.HBM)
            for x in (
                flow_state[0],
                forcing[0],
                jnp.transpose(pivot_table, (1, 2, 0, 3)),
                block_offset.reshape(1, stations),
                line_perm.reshape(1, radial),
                axial_jac,
                radial_jac,
                lower_block,
                upper_block,
            )
        )
    )
    anywhere = pl.BlockSpec(memory_space=pl.ANY)
    residual, correction = pl.pallas_call(
        deliver,
        out_shape=(block, block),
        in_specs=[vmem] * 2,
        out_specs=(anywhere, anywhere),
        scratch_shapes=[dma((2,))],
    )(
        pltpu.with_memory_space_constraint(residual, pltpu.VMEM),
        pltpu.with_memory_space_constraint(correction, pltpu.VMEM),
    )
    return residual[None], correction[None]


def solution(mesh):
    spec = P("inst", None, "space", None)
    return jax.shard_map(
        functools.partial(shards, mesh.shape["inst"], mesh.shape["space"]),
        mesh=mesh,
        in_specs=(spec, spec, P(), P("space"), P(), P(), P(), P(), P()),
        out_specs=(spec, spec),
        check_vma=False,
    )
```
